32 devices in a mesh: groups: 2 (over x), ctx: 8 (over z, y), head: 2 (over core).
Axes of the slice: x: 2, y: 2, z: 4, core: 2. Of those that a mesh axis runs over, the one named last changes fastest.
Arguments:
- queries: bfloat16 [4096, 20, 128], P(('groups', 'ctx'), 'head'), parts along dimension 0, may hold values from -70 to 70, as said below
- keys: bfloat16 [4096, 4, 128], P(('groups', 'ctx'), 'head'), parts along dimension 0, may hold values from -3.5 to 3.5
- doc_lengths: int32 [8], P('groups'), parts along dimension 0, may hold values from 1 to 24, 32 in all
- gate_query_weight: bfloat16 [20, 128, 128], P('head'), may hold values from -0.5 to 0.5
- gate_key_weight: bfloat16 [4, 384, 128], P('head'), may hold values from -0.3125 to 0.3125
Outputs:
- block_targets: float32 [20, 64, 32], P('head', ('groups', 'ctx')), parts along dimension 1
- key_proj_grad: float32 [64, 4, 128], P(('groups', 'ctx'), 'head'), parts along dimension 0
- query_weight_grad: float32 [40, 128, 128], P(('groups', 'head')), parts along dimension 0
- key_weight_grad: float32 [8, 384, 128], P(('groups', 'head')), parts along dimension 0
The draws below stay inside these ranges and needn't reach their ends.
There are 2 independent parts, one for each index of `groups`. The reference program is written for one: setup_inputs(seed, part) draws one part's arguments, and reference() takes and returns one part's arrays. A program takes and returns all parts, laid end to end along the dimension named above; an argument that names none is the same for every part. Nothing has to cross between parts.
Inputs may be any that keep to these rules, and one draw needn't show every extreme that they name: queries are of order one except in a few rows.
All inputs are finite; a program needn't handle non-finite values.
Results may differ from the reference program's by a relative error of at most 0.006.
Values may be sent and summed in bfloat16 or wider, within the bound.
No kernel may reach another device: no remote copies, remote signals or barrier semaphores. Data moves between devices by JAX's collectives and lax.ppermute only.
A program may use at most 64 MiB of HBM per device.

```python
import math
import jax
import jax.numpy as jnp
import numpy as np
from jax import lax

HEADS = 20
KV_HEADS = 4
HD = 128
GD = 128
BLK = 64
NDOCS = 4
SEQ = 2048
NBLK = 32


def key_field(key):
    key = jax.random.fold_in(key, 5)
    noise_key, common_key = jax.random.split(key)
    noise = jax.random.normal(noise_key, (SEQ // BLK, BLK, KV_HEADS, HD), jnp.float32)
    common = jax.random.normal(common_key, (SEQ // BLK, 1, KV_HEADS, HD), jnp.float32)
    return jnp.clip(0.7 * (noise + common), -3.5, 3.5).reshape(SEQ, KV_HEADS, HD)


def draw_keys(key, part):
    field = key_field(key)
    return field.astype(jnp.bfloat16)


def draw_queries(key, part):
    key = jax.random.fold_in(key, 17)
    noise_key, common_key = jax.random.split(key)
    noise = jax.random.normal(noise_key, (SEQ // BLK, BLK, HEADS, HD), jnp.float32)
    common = jax.random.normal(common_key, (SEQ // BLK, 1, HEADS, HD), jnp.float32)
    values = jnp.clip(0.7 * (noise + common), -3.5, 3.5).reshape(SEQ, HEADS, HD)
    return values.astype(jnp.bfloat16)


def block_levels(own_key, extent, shards, low, high):
    factor_of = 1.0
    for axis_at, parts in shards:
        draws = jax.random.uniform(jax.random.fold_in(jax.random.fold_in(own_key, 6), axis_at), (parts,), jnp.float32, low / len(shards), high / len(shards))
        factor_of = factor_of * jnp.repeat(jnp.exp(draws), extent[axis_at] // parts).reshape((-1,) + (1,) * (len(extent) - 1 - axis_at))
    return factor_of


def profile(amount, total, most, lean):
    weights = [(1 << 20) // math.isqrt(rank ** lean) + 1 for rank in range(2, amount + 1)]
    spare, given = total - most - (amount - 1), [1] * (amount - 1)
    while spare > 0:
        candidates = [i for i in range(amount - 1) if given[i] < most]
        pool, left = sum([weights[i] for i in candidates]), spare
        for i in candidates:
            addition = min(most - given[i], max(1, left * weights[i] // pool), spare)
            given[i] = given[i] + addition
            spare = spare - addition
    return np.array([most] + given)


def uneven(key, number_of, total, bound, lean):
    if number_of == 2:
        one = jax.random.randint(key, (), max(1, total - bound), min(bound, total - 1) + 1)
        return jnp.stack([one, total - one])
    sizes = jnp.asarray(profile(number_of, total, bound, lean), jnp.int32)
    couples = (number_of - 1) // 2
    source_of, taker = sizes[1:1 + 2 * couples:2], sizes[2:2 + 2 * couples:2]
    slack = jnp.minimum(source_of - 1, bound - taker)
    moved = jax.random.randint(jax.random.fold_in(key, 1), (couples,), 0, 1 << 20) % (slack + 1)
    sizes = sizes.at[1:1 + 2 * couples:2].set(source_of - moved).at[2:2 + 2 * couples:2].set(taker + moved)
    return sizes[jax.random.permutation(jax.random.fold_in(key, 2), number_of)]


def gaussian(rng, shape, width, bound, cuts=(), kind=jnp.bfloat16):
    gain = block_levels(rng, shape, cuts, -0.22, 0.18) if cuts else 1.0
    array = jax.random.normal(rng, shape, jnp.float32) * width * gain
    return jnp.minimum(jnp.maximum(array, -bound), bound).astype(kind)


def setup_inputs(seed: int = 0, part: int = 0) -> dict:
    key_of = jax.random.split(jax.random.key(seed), 6)
    part_keys = jax.random.split(jax.random.fold_in(key_of[5], part), 6)
    return {
        "queries": draw_queries(jax.random.fold_in(jax.random.fold_in(key_of[5], part), 71), part),
        "keys": draw_keys(jax.random.fold_in(jax.random.fold_in(key_of[5], part), 71), part),
        "doc_lengths": uneven(part_keys[2], NDOCS, NBLK, 3 * NBLK // 4, 2).astype(jnp.int32),
        "gate_query_weight": gaussian(key_of[3], (HEADS, HD, GD), HD ** -0.5, 0.5, ((0, 2),)),
        "gate_key_weight": gaussian(key_of[4], (KV_HEADS, 3 * HD, GD), (3 * HD) ** -0.5, 0.3125, ((0, 2),)),
    }


def doc_block_starts(doc_lengths, block_count):
    doc_ends = jnp.cumsum(doc_lengths)
    doc_begins = doc_ends - doc_lengths
    block_ids = jnp.arange(block_count, dtype=jnp.int32)
    return lax.optimization_barrier(jnp.max(jnp.where(doc_begins[None, :] <= block_ids[:, None], doc_begins[None, :], 0), axis=1))

def reference(queries, keys, doc_lengths, gate_query_weight, gate_key_weight):
    seq_len = queries.shape[0]
    block_count = seq_len // BLK
    repeats = HEADS // KV_HEADS
    doc_start = doc_block_starts(doc_lengths, block_count)
    block_ids = jnp.arange(block_count, dtype=jnp.int32)
    row_ids = jnp.arange(seq_len, dtype=jnp.int32)
    lowest = doc_start[row_ids // BLK] * BLK
    allowed = (row_ids[None, :] <= row_ids[:, None]) & (row_ids[None, :] >= lowest[:, None])
    block_mask = (block_ids[None, :] <= block_ids[:, None]) & (block_ids[None, :] >= doc_start[:, None])
    score_scale = 1.0 / math.sqrt(HD)
    gate_scale = 1.0 / math.sqrt(GD)

    def one_head(head_id):
        query_rows = lax.dynamic_index_in_dim(queries, head_id, 1, keepdims=False).astype(jnp.float32)
        key_rows = lax.dynamic_index_in_dim(keys, head_id // repeats, 1, keepdims=False).astype(jnp.float32)
        scores = jnp.dot(query_rows, key_rows.T, precision=lax.Precision.HIGHEST) * score_scale
        scores = jnp.where(allowed, scores, -jnp.inf)
        row_max = lax.optimization_barrier(jnp.max(scores, axis=1))
        log_total = row_max + jnp.log(lax.optimization_barrier(jnp.sum(jnp.exp(scores - row_max[:, None]), axis=1)))
        block_best = lax.optimization_barrier(jnp.max(scores.reshape(seq_len, block_count, BLK), axis=2))
        ratios = jnp.exp(block_best - log_total[:, None]).reshape(block_count, BLK, block_count).max(1)
        ratios = jnp.where(block_mask, ratios, 0.0)
        return ratios / lax.optimization_barrier(jnp.sum(ratios, axis=1, keepdims=True))
    block_targets = lax.map(one_head, jnp.arange(HEADS, dtype=jnp.int32))
    pooled_q = queries.astype(jnp.float32).reshape(block_count, BLK, HEADS, HD).mean(1).astype(jnp.bfloat16)
    key_blocks = keys.astype(jnp.float32).reshape(block_count, BLK, KV_HEADS, HD)
    pooled_k = jnp.concatenate([key_blocks.max(1), key_blocks.min(1), key_blocks.mean(1)], axis=-1).astype(jnp.bfloat16)
    query_proj = jnp.einsum('ahd,hde->ahe', pooled_q.astype(jnp.float32), gate_query_weight.astype(jnp.float32), precision=lax.Precision.HIGHEST)
    key_proj = jnp.einsum('cgd,gde->cge', pooled_k.astype(jnp.float32), gate_key_weight.astype(jnp.float32), precision=lax.Precision.HIGHEST)
    proj_split = query_proj.reshape(block_count, KV_HEADS, repeats, GD)
    logits = jnp.einsum('agre,cge->grac', proj_split, key_proj, precision=lax.Precision.HIGHEST).reshape(HEADS, block_count, block_count) * gate_scale
    logits = jnp.where(block_mask[None], logits, -jnp.inf)
    gate_exp = jnp.exp(logits - lax.optimization_barrier(jnp.max(logits, axis=-1, keepdims=True)))
    gate_probs = gate_exp / lax.optimization_barrier(jnp.sum(gate_exp, axis=-1, keepdims=True))
    delta = jnp.where(block_mask[None], gate_probs - block_targets, 0.0)
    delta_split = delta.reshape(KV_HEADS, repeats, block_count, block_count)
    query_grad = jnp.einsum('grac,cge->agre', delta_split, key_proj, precision=lax.Precision.HIGHEST).reshape(block_count, HEADS, GD) * gate_scale
    query_weight_grad = jnp.einsum('ahd,ahe->hde', pooled_q.astype(jnp.float32), query_grad, precision=lax.Precision.HIGHEST)
    key_proj_grad = jnp.einsum('grac,agre->cge', delta_split, proj_split, precision=lax.Precision.HIGHEST) * gate_scale
    key_weight_grad = jnp.einsum('cgd,cge->gde', pooled_k.astype(jnp.float32), key_proj_grad, precision=lax.Precision.HIGHEST)
    return (block_targets, key_proj_grad, query_weight_grad, key_weight_grad)
```

```python
import functools
import math

import jax
import jax.numpy as jnp
from jax import lax
from jax.experimental import pallas as pl
from jax.experimental.pallas import tpu as pltpu
from jax.sharding import PartitionSpec as P

BLK = 64
LOG2E = 1.4426950408889634
LOW = -1e30
VMEM_LIMIT = 60 * 1024 * 1024
F32 = jnp.float32
BF16 = jnp.bfloat16


def dot(a, b, a_dim, b_dim, precision=None):
    return lax.dot_general(
        a, b, (((a_dim,), (b_dim,)), ((), ())), precision=precision, preferred_element_type=F32
    )


def exact_dot(a, b, a_dim, b_dim):
    return dot(a, b, a_dim, b_dim, lax.Precision.HIGHEST)


def doc_begins(lengths_ref):
    begins, total = [], jnp.int32(0)
    for doc in range(lengths_ref.shape[0]):
        begins.append(total)
        total = total + lengths_ref[doc]
    return begins


def start_of(begins, block):
    start = jnp.zeros_like(block)
    for begin in begins:
        start = jnp.maximum(start, jnp.where(begin <= block, begin, 0))
    return start


def prep_kernel(q_ref, k_ref, packed_ref):
    rows, width = k_ref.shape
    heads, _, head_size = q_ref.shape
    blocks = rows // BLK
    per_row = width // head_size
    packed_ref[0:rows, :] = k_ref[...]
    pooled = []
    for head in range(heads):
        values = q_ref[head].astype(F32).reshape(blocks, BLK, head_size)
        pooled.append(jnp.sum(values, axis=1) * (1.0 / BLK))
    lines = [
        jnp.concatenate(pooled[at : at + per_row], axis=1) for at in range(0, heads, per_row)
    ]
    spare = packed_ref.shape[0] - rows - blocks * len(lines)
    lines.append(jnp.zeros((spare, width), F32))
    packed_ref[rows:, :] = jnp.concatenate(lines, axis=0).astype(BF16)


def attention_kernel(scale, ranks, lengths_ref, q_ref, *refs):
    pieces = refs[:ranks]
    targets_ref, sent_ref, pooled_q_ref, pooled_k_ref = refs[ranks : ranks + 4]
    best_ref, sum_ref, pk_ref, pq_ref = refs[ranks + 4 :]
    heads, rows, head_size = q_ref.shape
    width = pieces[0].shape[1]
    kv = width // head_size
    repeats = heads // kv
    blocks = rows // BLK
    block_count = blocks * ranks
    me = lax.axis_index("ctx")
    begins = doc_begins(lengths_ref)
    first_needed = start_of(begins, me * blocks)
    causal = lax.broadcasted_iota(jnp.int32, (rows, rows), 0) <= lax.broadcasted_iota(
        jnp.int32, (rows, rows), 1
    )

    for step in range(ranks):
        piece = pieces[step]
        source = me ^ step
        keys = piece[0:rows, :].astype(F32).reshape(blocks, BLK, width)
        stats = (jnp.max(keys, 1), jnp.min(keys, 1), jnp.sum(keys, 1) * (1.0 / BLK))
        for group in range(kv):
            for at, value in enumerate(stats):
                pk_ref[group, source, :, at * head_size : (at + 1) * head_size] = value[
                    :, group * head_size : (group + 1) * head_size
                ]
        tail = piece[rows:, :].astype(F32)
        for head in range(heads):
            line, part = head // kv, head % kv
            pq_ref[head, source] = tail[
                line * blocks : (line + 1) * blocks, part * head_size : (part + 1) * head_size
            ]

        @pl.when((source <= me) & (source * blocks + blocks > first_needed))
        def _(step=step, piece=piece, source=source):
            for group in range(kv):
                key_rows = piece[0:rows, group * head_size : (group + 1) * head_size]
                for head in range(group * repeats, (group + 1) * repeats):
                    scores = dot(key_rows, q_ref[head], 1, 1)
                    if step == 0:
                        scores = jnp.where(causal, scores, LOW)
                    scores = scores.reshape(blocks, BLK, rows)
                    best = jnp.max(scores, axis=1)
                    total = jnp.sum(jnp.exp2((scores - best[:, None, :]) * scale), axis=1)
                    best_ref[head, source] = best
                    sum_ref[head, source] = total

    shape = (ranks, blocks, rows)
    key_block = lax.broadcasted_iota(jnp.int32, shape, 0) * blocks + lax.broadcasted_iota(
        jnp.int32, shape, 1
    )
    query_block = me * blocks + lax.broadcasted_iota(jnp.int32, shape, 2) // BLK
    valid = (key_block <= query_block) & (key_block >= start_of(begins, query_block))
    lane = lax.broadcasted_iota(jnp.int32, (ranks, blocks, 128), 2)
    gathered = jnp.zeros((ranks, blocks, 128), F32)
    for head in range(heads):
        best = jnp.where(valid, best_ref[head], LOW)
        top = jnp.max(jnp.max(best, axis=0, keepdims=True), axis=1, keepdims=True)
        shifted = (best - top) * scale
        total = jnp.where(valid, sum_ref[head] * jnp.exp2(shifted), 0.0)
        total = jnp.sum(jnp.sum(total, axis=0, keepdims=True), axis=1, keepdims=True)
        ratio = jnp.where(valid, shifted - jnp.log2(total), LOW)
        for block in range(blocks):
            part = ratio[:, :, block * BLK // 128 * 128 : (block * BLK // 128 + 1) * 128]
            inside = (lane // BLK) == (block % (128 // BLK))
            high = jnp.max(jnp.where(inside, part, LOW), axis=2, keepdims=True)
            gathered = jnp.where(lane == head * blocks + block, high, gathered)
    raw = jnp.exp2(gathered)
    norm = jnp.sum(jnp.sum(raw, axis=0, keepdims=True), axis=1, keepdims=True)
    final = (raw / norm).reshape(block_count, 128)
    if block_count < 128:
        final = jnp.concatenate([final, jnp.zeros((128 - block_count, 128), F32)], axis=0)
    final = final.T
    sent_ref[...] = final[0 : heads * blocks]
    for head in range(heads):
        targets_ref[head] = final[head * blocks : (head + 1) * blocks, 0:block_count]
        pooled_q_ref[head] = pq_ref[head].reshape(block_count, head_size).astype(BF16)
    for group in range(kv):
        pooled_k_ref[group] = pk_ref[group].reshape(block_count, 3 * head_size).astype(BF16)


def gate_kernel(
    scale,
    ranks,
    lengths_ref,
    all_targets_ref,
    pooled_q_ref,
    pooled_k_ref,
    wq_ref,
    wk_ref,
    key_grad_ref,
    wq_grad_ref,
    wk_grad_ref,
    own_ref,
):
    heads, block_count, head_size = pooled_q_ref.shape
    kv = pooled_k_ref.shape[0]
    repeats = heads // kv
    blocks = block_count // ranks
    me = lax.axis_index("ctx")
    begins = doc_begins(lengths_ref)
    shape = (repeats * block_count, block_count)
    query_block = lax.broadcasted_iota(jnp.int32, shape, 0) % block_count
    key_block = lax.broadcasted_iota(jnp.int32, shape, 1)
    valid = (key_block <= query_block) & (key_block >= start_of(begins, query_block))
    for group in range(kv):
        members = range(group * repeats, (group + 1) * repeats)
        pooled_k = pooled_k_ref[group]
        key_proj = dot(pooled_k, wk_ref[group], 1, 0)
        query_proj = jnp.concatenate(
            [dot(pooled_q_ref[head], wq_ref[head], 1, 0) for head in members], axis=0
        )
        logits = jnp.where(valid, exact_dot(query_proj, key_proj, 1, 1) * scale, LOW)
        weights = jnp.exp(logits - jnp.max(logits, axis=1, keepdims=True))
        probs = weights / jnp.sum(weights, axis=1, keepdims=True)
        targets = jnp.concatenate(
            [
                all_targets_ref[:, head * blocks : (head + 1) * blocks, :].reshape(block_count, 128)[
                    :, 0:block_count
                ]
                for head in members
            ],
            axis=0,
        )
        delta = jnp.where(valid, probs - targets, 0.0)
        query_grad = exact_dot(delta, key_proj, 1, 0) * scale
        key_grad = exact_dot(delta, query_proj, 0, 0) * scale
        for at, head in enumerate(members):
            wq_grad_ref[head] = exact_dot(
                pooled_q_ref[head].astype(F32),
                query_grad[at * block_count : (at + 1) * block_count],
                0,
                0,
            )
        wk_grad_ref[group] = exact_dot(pooled_k.astype(F32), key_grad, 0, 0)
        own_ref[...] = key_grad.reshape(ranks, blocks, head_size)
        key_grad_ref[:, group, :] = own_ref[me]


def per_device(queries, keys, doc_lengths, gate_query_weight, gate_key_weight):
    rows, heads, head_size = queries.shape
    kv = keys.shape[1]
    ranks = lax.axis_size("ctx")
    blocks = rows // BLK
    block_count = blocks * ranks
    width = kv * head_size
    extra = -(-(blocks * heads // kv) // 16) * 16
    params = pltpu.CompilerParams(vmem_limit_bytes=VMEM_LIMIT)
    smem = pl.BlockSpec(memory_space=pltpu.SMEM)
    vmem = pl.BlockSpec(memory_space=pltpu.VMEM)

    head_queries = queries.transpose(1, 0, 2)
    flat_keys = keys.reshape(rows, width)
    packed = pl.pallas_call(
        prep_kernel,
        out_shape=jax.ShapeDtypeStruct((rows + extra, width), BF16),
        in_specs=[vmem, vmem],
        out_specs=vmem,
        compiler_params=params,
        name="pool_queries",
    )(head_queries, flat_keys)
    pieces = [packed] + [
        lax.ppermute(packed, "ctx", [(i, i ^ step) for i in range(ranks)])
        for step in range(1, ranks)
    ]
    block_targets, sent, pooled_q, pooled_k = pl.pallas_call(
        functools.partial(attention_kernel, LOG2E / math.sqrt(head_size), ranks),
        out_shape=(
            jax.ShapeDtypeStruct((heads, blocks, block_count), F32),
            jax.ShapeDtypeStruct((heads * blocks, 128), F32),
            jax.ShapeDtypeStruct((heads, block_count, head_size), BF16),
            jax.ShapeDtypeStruct((kv, block_count, 3 * head_size), BF16),
        ),
        in_specs=[smem] + [vmem] * (1 + ranks),
        out_specs=(vmem,) * 4,
        scratch_shapes=[
            pltpu.VMEM((heads, ranks, blocks, rows), F32),
            pltpu.VMEM((heads, ranks, blocks, rows), F32),
            pltpu.VMEM((kv, ranks, blocks, 3 * head_size), F32),
            pltpu.VMEM((heads, ranks, blocks, head_size), F32),
        ],
        compiler_params=params,
        name="block_max_attention",
    )(doc_lengths, head_queries, *pieces)
    all_targets = lax.all_to_all(
        jnp.broadcast_to(sent[None], (ranks,) + sent.shape), "ctx", 0, 0
    )
    key_proj_grad, query_weight_grad, key_weight_grad = pl.pallas_call(
        functools.partial(gate_kernel, 1.0 / math.sqrt(gate_query_weight.shape[2]), ranks),
        out_shape=(
            jax.ShapeDtypeStruct((blocks, kv, head_size), F32),
            jax.ShapeDtypeStruct(gate_query_weight.shape, F32),
            jax.ShapeDtypeStruct(gate_key_weight.shape, F32),
        ),
        in_specs=[smem] + [vmem] * 5,
        out_specs=(vmem,) * 3,
        scratch_shapes=[pltpu.VMEM((ranks, blocks, head_size), F32)],
        compiler_params=params,
        name="gate_gradients",
    )(doc_lengths, all_targets, pooled_q, pooled_k, gate_query_weight, gate_key_weight)
    return (block_targets, key_proj_grad, query_weight_grad, key_weight_grad)


def solution(mesh):
    placed = (
        P(("groups", "ctx"), "head", None),
        P(("groups", "ctx"), "head", None),
        P("groups"),
        P("head", None, None),
        P("head", None, None),
    )
    return jax.shard_map(
        per_device,
        mesh=mesh,
        in_specs=placed,
        out_specs=(
            P("head", ("groups", "ctx"), None),
            P(("groups", "ctx"), "head", None),
            P(("groups", "head"), None, None),
            P(("groups", "head"), None, None),
        ),
        check_vma=False,
    )
```

```python
import functools
import math

import jax
import jax.numpy as jnp
from jax import lax
from jax.experimental import pallas as pl
from jax.experimental.pallas import tpu as pltpu
from jax.sharding import PartitionSpec as P

BLK = 64
LANES = 128
LOG2E = 1.4426950408889634
LOW = -1e30
VMEM_LIMIT = 60 * 1024 * 1024
F32 = jnp.float32
BF16 = jnp.bfloat16


def dot(a, b, a_dim, b_dim, precision=None):
    return lax.dot_general(
        a, b, (((a_dim,), (b_dim,)), ((), ())), precision=precision, preferred_element_type=F32
    )


def halves(value):
    high = value.astype(BF16)
    return high, (value - high.astype(F32)).astype(BF16)


def iota(shape, dim):
    return lax.broadcasted_iota(jnp.int32, shape, dim)


def doc_begins(lengths_ref):
    begins, total = [], jnp.int32(0)
    for doc in range(lengths_ref.shape[0]):
        begins.append(total)
        total = total + lengths_ref[doc]
    return begins


def start_of(begins, block):
    start = jnp.zeros_like(block)
    for begin in begins:
        start = jnp.maximum(start, jnp.where(begin <= block, begin, 0))
    return start


def pool_keys(piece_ref, out_ref, at, head_size):
    rows, width = piece_ref.shape
    keys = piece_ref[...].astype(F32).reshape(rows // BLK, BLK, width)
    stats = (jnp.max(keys, 1), jnp.min(keys, 1), jnp.sum(keys, 1) * (1.0 / BLK))
    for group in range(width // head_size):
        for part, value in enumerate(stats):
            out_ref[group, at, :, part * head_size : (part + 1) * head_size] = value[
                :, group * head_size : (group + 1) * head_size
            ]


def absorb(scale, begins, me, step, piece_ref, q_ref, best_ref, sum_ref, at):
    heads, rows, head_size = q_ref.shape
    kv = piece_ref.shape[1] // head_size
    blocks = rows // BLK
    source = me ^ step
    needed = (source <= me) & (source * blocks + blocks > start_of(begins, me * blocks))

    @pl.when(needed)
    def _():
        if step == 0:
            causal = iota((rows, rows), 0) <= iota((rows, rows), 1)
        for head in range(heads):
            group = head // (heads // kv)
            key_rows = piece_ref[:, group * head_size : (group + 1) * head_size]
            scores = dot(key_rows, q_ref[head], 1, 1)
            if step == 0:
                scores = jnp.where(causal, scores, LOW)
            scores = scores.reshape(blocks, BLK, rows)
            best = jnp.max(scores, axis=1)
            best_ref[head, at] = best
            sum_ref[head, at] = jnp.sum(jnp.exp2((scores - best[:, None, :]) * scale), axis=1)


def early_kernel(scale, steps, lengths_ref, q_ref, wq_ref, *refs):
    pieces = refs[: len(steps)]
    best_ref, sum_ref, pk_ref, pq_ref, proj_ref = refs[len(steps) :]
    heads, rows, head_size = q_ref.shape
    blocks = rows // BLK
    me = lax.axis_index("ctx")
    begins = doc_begins(lengths_ref)
    for head in range(heads):
        values = q_ref[head].astype(F32).reshape(blocks, BLK, head_size)
        pooled = (jnp.sum(values, axis=1) * (1.0 / BLK)).astype(BF16)
        pq_ref[head * blocks : (head + 1) * blocks, :] = pooled.astype(F32)
        proj_ref[head * blocks : (head + 1) * blocks, :] = dot(pooled, wq_ref[head], 1, 0)
    for at, (step, piece_ref) in enumerate(zip(steps, pieces)):
        pool_keys(piece_ref, pk_ref, at, head_size)
        absorb(scale, begins, me, step, piece_ref, q_ref, best_ref, sum_ref, at)


def late_kernel(scale, gate_scale, early_steps, late_steps, lengths_ref, q_ref, wk_ref, *refs):
    count = len(late_steps)
    pieces = refs[:count]
    best_ref, sum_ref, pk_ref, pq_ref, proj_ref = refs[count : count + 5]
    targets_ref, sent_ref, pooled_k_ref, key_proj_ref = refs[count + 5 : count + 9]
    late_best_ref, late_sum_ref, late_pk_ref, all_pk_ref, column_ref = refs[count + 9 :]
    heads, rows, head_size = q_ref.shape
    kv = wk_ref.shape[0]
    blocks = rows // BLK
    ranks = len(early_steps) + count
    block_count = blocks * ranks
    own_rows = heads * blocks
    me = lax.axis_index("ctx")
    begins = doc_begins(lengths_ref)
    for at, (step, piece_ref) in enumerate(zip(late_steps, pieces)):
        pool_keys(piece_ref, late_pk_ref, at, head_size)
        absorb(scale, begins, me, step, piece_ref, q_ref, late_best_ref, late_sum_ref, at)

    steps = tuple(early_steps) + tuple(late_steps)
    for group in range(kv):
        for at, step in enumerate(early_steps):
            all_pk_ref[group, me ^ step] = pk_ref[group, at]
        for at, step in enumerate(late_steps):
            all_pk_ref[group, me ^ step] = late_pk_ref[group, at]
    proj = proj_ref[...]
    logits = jnp.zeros((own_rows, block_count), F32)
    row = iota((own_rows, block_count), 0)
    for group in range(kv):
        pooled_k = all_pk_ref[group].reshape(block_count, 3 * head_size).astype(BF16)
        key_proj = dot(pooled_k, wk_ref[group], 1, 0)
        pooled_k_ref[group] = pooled_k
        key_proj_ref[group] = key_proj
        part = dot(proj, key_proj, 1, 1, lax.Precision.HIGHEST)
        logits = jnp.where(row // (own_rows // kv) == group, part, logits)
    query_block = me * blocks + row % blocks
    key_block = iota((own_rows, block_count), 1)
    allowed = (key_block <= query_block) & (key_block >= start_of(begins, query_block))
    logits = jnp.where(allowed, logits * gate_scale, LOW)
    weights = jnp.exp(logits - jnp.max(logits, axis=1, keepdims=True))
    probs = weights / jnp.sum(weights, axis=1, keepdims=True)

    lane_block = me * blocks + iota((blocks, rows), 1) // BLK
    lane_start = start_of(begins, lane_block)
    valid = []
    for step in steps:
        key_block = (me ^ step) * blocks + iota((blocks, rows), 0)
        valid.append((key_block <= lane_block) & (key_block >= lane_start))
    lane = iota((blocks, LANES), 1)
    columns = [jnp.zeros((blocks, LANES), F32) for _ in steps]
    for head in range(heads):
        best = [best_ref[head, at] for at in range(len(early_steps))]
        best += [late_best_ref[head, at] for at in range(count)]
        total = [sum_ref[head, at] for at in range(len(early_steps))]
        total += [late_sum_ref[head, at] for at in range(count)]
        best = [jnp.where(ok, value, LOW) for ok, value in zip(valid, best)]
        top = jnp.max(functools.reduce(jnp.maximum, best), axis=0, keepdims=True)
        shifted = [(value - top) * scale for value in best]
        total = [
            jnp.where(ok, value * jnp.exp2(shift), 0.0)
            for ok, value, shift in zip(valid, total, shifted)
        ]
        lse = jnp.log2(jnp.sum(functools.reduce(jnp.add, total), axis=0, keepdims=True))
        for at in range(ranks):
            ratio = jnp.where(valid[at], shifted[at] - lse, LOW)
            for block in range(blocks):
                tile = block * BLK // LANES
                inside = (lane // BLK) == (block % (LANES // BLK))
                part = jnp.where(inside, ratio[:, tile * LANES : (tile + 1) * LANES], LOW)
                high = jnp.max(part, axis=1, keepdims=True)
                columns[at] = jnp.where(lane == head * blocks + block, high, columns[at])
    raw = [jnp.exp2(value) for value in columns]
    norm = 1.0 / jnp.sum(functools.reduce(jnp.add, raw), axis=0, keepdims=True)
    for at, step in enumerate(steps):
        column_ref[me ^ step] = raw[at] * norm
    final = column_ref[...].reshape(block_count, LANES)
    if block_count < LANES:
        final = jnp.concatenate([final, jnp.zeros((LANES - block_count, LANES), F32)], axis=0)
    targets = final.T[0:own_rows, 0:block_count]
    for head in range(heads):
        targets_ref[head] = targets[head * blocks : (head + 1) * blocks]

    delta = jnp.where(allowed, probs - targets, 0.0)
    high, low = halves(delta)
    pieces_of_row = [high.astype(F32), low.astype(F32)]
    width = sent_ref.shape[2]
    if width > 2 * block_count:
        pieces_of_row.append(jnp.zeros((own_rows, width - 2 * block_count), F32))
    pooled_q = pq_ref[...]
    if width > head_size:
        pooled_q = jnp.concatenate(
            [pooled_q, jnp.zeros((own_rows, width - head_size), F32)], axis=1
        )
    packed = jnp.concatenate([pooled_q, jnp.concatenate(pieces_of_row, axis=1)], axis=0)
    packed = packed.astype(BF16)
    for rank in range(ranks):
        sent_ref[rank] = packed


def gate_kernel(
    scale, packed_ref, pooled_k_ref, key_proj_ref, wq_ref, key_grad_ref, wq_grad_ref, wk_grad_ref,
    own_ref,
):
    ranks, packed_rows, _ = packed_ref.shape
    kv, block_count, _ = pooled_k_ref.shape
    heads, head_size, _ = wq_ref.shape
    repeats = heads // kv
    blocks = block_count // ranks
    me = lax.axis_index("ctx")
    packed = packed_ref[...].astype(F32)
    for group in range(kv):
        key_high, key_low = halves(key_proj_ref[group] * scale)
        both_keys = jnp.concatenate([key_high, key_high], axis=0)
        pooled, deltas, projected = [], [], []
        for head in range(group * repeats, (group + 1) * repeats):
            rows = packed[:, head * blocks : (head + 1) * blocks, 0:head_size]
            pooled.append(rows.reshape(block_count, head_size).astype(BF16))
            at = packed_rows // 2 + head * blocks
            rows = packed[:, at : at + blocks, :].reshape(block_count, -1)
            deltas.append(rows[:, 0 : 2 * block_count].astype(BF16))
            projected.append(dot(pooled[-1], wq_ref[head], 1, 0))
        delta = jnp.concatenate(deltas, axis=0)
        delta_high = delta[:, 0:block_count]
        query_grad = dot(delta, both_keys, 1, 0) + dot(delta_high, key_low, 1, 0)
        grad_high, grad_low = halves(query_grad)
        for at in range(repeats):
            rows = slice(at * block_count, (at + 1) * block_count)
            wq_grad_ref[group * repeats + at] = dot(
                jnp.concatenate([pooled[at], pooled[at]], axis=0),
                jnp.concatenate([grad_high[rows], grad_low[rows]], axis=0),
                0,
                0,
            )
        proj_high, proj_low = halves(jnp.concatenate(projected, axis=0) * scale)
        main = dot(delta, proj_high, 0, 0)
        key_grad = main[0:block_count] + main[block_count:] + dot(delta_high, proj_low, 0, 0)
        grad_high, grad_low = halves(key_grad)
        pooled_k = pooled_k_ref[group]
        wk_grad_ref[group] = dot(
            jnp.concatenate([pooled_k, pooled_k], axis=0),
            jnp.concatenate([grad_high, grad_low], axis=0),
            0,
            0,
        )
        own_ref[...] = key_grad.reshape(ranks, blocks, head_size)
        key_grad_ref[:, group, :] = own_ref[me]


def per_device(queries, keys, doc_lengths, gate_query_weight, gate_key_weight):
    rows, heads, head_size = queries.shape
    kv = keys.shape[1]
    ranks = lax.axis_size("ctx")
    blocks = rows // BLK
    block_count = blocks * ranks
    own_rows = heads * blocks
    scale = LOG2E / math.sqrt(head_size)
    gate_scale = 1.0 / math.sqrt(gate_query_weight.shape[2])
    params = pltpu.CompilerParams(vmem_limit_bytes=VMEM_LIMIT)
    smem = pl.BlockSpec(memory_space=pltpu.SMEM)
    vmem = pl.BlockSpec(memory_space=pltpu.VMEM)

    def exchange(value, step):
        return lax.ppermute(value, "ctx", [(i, i ^ step) for i in range(ranks)])

    flat_keys = keys.reshape(rows, kv * head_size)
    early_steps = [0, 1] + list(range(2, ranks, 2))
    late_steps = list(range(3, ranks, 2))
    pieces = {0: flat_keys}
    for step in early_steps[1:]:
        pieces[step] = exchange(flat_keys, step)
    for step in late_steps:
        pieces[step] = exchange(pieces[step - 1], 1)

    head_queries = queries.transpose(1, 0, 2)
    stats = jax.ShapeDtypeStruct((heads, len(early_steps), blocks, rows), F32)
    late_stats = pltpu.VMEM((heads, max(len(late_steps), 1), blocks, rows), F32)
    early = pl.pallas_call(
        functools.partial(early_kernel, scale, early_steps),
        out_shape=(
            stats,
            stats,
            jax.ShapeDtypeStruct((kv, len(early_steps), blocks, 3 * head_size), F32),
            jax.ShapeDtypeStruct((own_rows, head_size), F32),
            jax.ShapeDtypeStruct((own_rows, head_size), F32),
        ),
        in_specs=[smem] + [vmem] * (2 + len(early_steps)),
        out_specs=(vmem,) * 5,
        compiler_params=params,
        name="early_key_blocks",
    )(doc_lengths, head_queries, gate_query_weight, *[pieces[s] for s in early_steps])
    width = -(-2 * block_count // LANES) * LANES
    block_targets, sent, pooled_k, key_proj = pl.pallas_call(
        functools.partial(late_kernel, scale, gate_scale, early_steps, late_steps),
        out_shape=(
            jax.ShapeDtypeStruct((heads, blocks, block_count), F32),
            jax.ShapeDtypeStruct((ranks, 2 * own_rows, width), BF16),
            jax.ShapeDtypeStruct((kv, block_count, 3 * head_size), BF16),
            jax.ShapeDtypeStruct((kv, block_count, head_size), F32),
        ),
        in_specs=[smem] + [vmem] * (7 + len(late_steps)),
        out_specs=(vmem,) * 4,
        scratch_shapes=[
            late_stats,
            late_stats,
            pltpu.VMEM((kv, max(len(late_steps), 1), blocks, 3 * head_size), F32),
            pltpu.VMEM((kv, ranks, blocks, 3 * head_size), F32),
            pltpu.VMEM((ranks, blocks, LANES), F32),
        ],
        compiler_params=params,
        name="late_key_blocks",
    )(doc_lengths, head_queries, gate_key_weight, *[pieces[s] for s in late_steps], *early)
    packed = lax.all_to_all(sent, "ctx", 0, 0)
    key_proj_grad, query_weight_grad, key_weight_grad = pl.pallas_call(
        functools.partial(gate_kernel, gate_scale),
        out_shape=(
            jax.ShapeDtypeStruct((blocks, kv, head_size), F32),
            jax.ShapeDtypeStruct(gate_query_weight.shape, F32),
            jax.ShapeDtypeStruct(gate_key_weight.shape, F32),
        ),
        in_specs=[vmem] * 4,
        out_specs=(vmem,) * 3,
        scratch_shapes=[pltpu.VMEM((ranks, blocks, head_size), F32)],
        compiler_params=params,
        name="gate_gradients",
    )(packed, pooled_k, key_proj, gate_query_weight)
    return (block_targets, key_proj_grad, query_weight_grad, key_weight_grad)


def solution(mesh):
    placed = (
        P(("groups", "ctx"), "head", None),
        P(("groups", "ctx"), "head", None),
        P("groups"),
        P("head", None, None),
        P("head", None, None),
    )
    return jax.shard_map(
        per_device,
        mesh=mesh,
        in_specs=placed,
        out_specs=(
            P("head", ("groups", "ctx"), None),
            P(("groups", "ctx"), "head", None),
            P(("groups", "head"), None, None),
            P(("groups", "head"), None, None),
        ),
        check_vma=False,
    )
```

```python
import functools
import math

import jax
import jax.numpy as jnp
from jax import lax
from jax.experimental import pallas as pl
from jax.experimental.pallas import tpu as pltpu
from jax.sharding import PartitionSpec as P

BLK = 64
LANES = 128
LOG2E = 1.4426950408889634
LOW = -1e30
VMEM_LIMIT = 24 * 1024 * 1024
F32 = jnp.float32
BF16 = jnp.bfloat16


def dot(a, b, a_dim, b_dim, precision=None):
    return lax.dot_general(
        a, b, (((a_dim,), (b_dim,)), ((), ())), precision=precision, preferred_element_type=F32
    )


def halves(value):
    high = value.astype(BF16)
    return high, (value - high.astype(F32)).astype(BF16)


def iota(shape, dim):
    return lax.broadcasted_iota(jnp.int32, shape, dim)


def doc_begins(lengths_ref):
    begins, total = [], jnp.int32(0)
    for doc in range(lengths_ref.shape[0]):
        begins.append(total)
        total = total + lengths_ref[doc]
    return begins


def start_of(begins, block):
    start = jnp.zeros_like(block)
    for begin in begins:
        start = jnp.maximum(start, jnp.where(begin <= block, begin, 0))
    return start


def pool_keys(piece_ref, out_ref, at, head_size):
    rows, width = piece_ref.shape
    keys = piece_ref[...].astype(F32).reshape(rows // BLK, BLK, width)
    stats = (jnp.max(keys, 1), jnp.min(keys, 1), jnp.sum(keys, 1) * (1.0 / BLK))
    for group in range(width // head_size):
        for part, value in enumerate(stats):
            out_ref[group, at, :, part * head_size : (part + 1) * head_size] = value[
                :, group * head_size : (group + 1) * head_size
            ]


def absorb(scale, begins, me, step, piece_ref, q_ref, best_ref, sum_ref, at):
    heads, rows, head_size = q_ref.shape
    kv = piece_ref.shape[1] // head_size
    blocks = rows // BLK
    source = me ^ step
    needed = (source <= me) & (source * blocks + blocks > start_of(begins, me * blocks))

    @pl.when(needed)
    def _():
        if step == 0:
            causal = iota((rows, rows), 0) <= iota((rows, rows), 1)
        for head in range(heads):
            group = head // (heads // kv)
            key_rows = piece_ref[:, group * head_size : (group + 1) * head_size]
            scores = dot(key_rows, q_ref[head], 1, 1)
            if step == 0:
                scores = jnp.where(causal, scores, LOW)
            scores = scores.reshape(blocks, BLK, rows)
            best = jnp.max(scores, axis=1)
            best_ref[head, at : at + blocks, :] = best
            sum_ref[head, at : at + blocks, :] = jnp.sum(
                jnp.exp2((scores - best[:, None, :]) * scale), axis=1
            )


def own_kernel(
    scale, lengths_ref, far_q_ref, far_wq_ref, own_ref, side_ref,
    q_ref, wq_ref, best_ref, sum_ref, pk_ref, pq_ref, proj_ref, ready_ref, copied,
):
    heads, rows, head_size = q_ref.shape
    blocks = rows // BLK
    me = lax.axis_index("ctx")
    begins = doc_begins(lengths_ref)
    q_copy = pltpu.make_async_copy(far_q_ref, q_ref, copied.at[0])
    wq_copy = pltpu.make_async_copy(far_wq_ref, wq_ref, copied.at[1])
    q_copy.start()
    wq_copy.start()
    ready_ref[...] = jnp.zeros_like(ready_ref)
    pool_keys(own_ref, pk_ref, 0, head_size)
    pool_keys(side_ref, pk_ref, 1, head_size)
    q_copy.wait()
    wq_copy.wait()
    for head in range(heads):
        values = q_ref[head].astype(F32).reshape(blocks, BLK, head_size)
        pooled = (jnp.sum(values, axis=1) * (1.0 / BLK)).astype(BF16)
        pq_ref[head * blocks : (head + 1) * blocks, :] = pooled.astype(F32)
        proj_ref[head * blocks : (head + 1) * blocks, :] = dot(pooled, wq_ref[head], 1, 0)
    absorb(scale, begins, me, 0, own_ref, q_ref, best_ref, sum_ref, 0)
    absorb(scale, begins, me, 1, side_ref, q_ref, best_ref, sum_ref, blocks)


def pass_kernel(ready_ref, *refs):
    del ready_ref, refs


def direct_kernel(scale, steps, lengths_ref, q_ref, *refs):
    pieces = refs[: len(steps)]
    best_ref, sum_ref, pk_ref = refs[len(steps) :]
    _, rows, head_size = q_ref.shape
    blocks = rows // BLK
    me = lax.axis_index("ctx")
    begins = doc_begins(lengths_ref)
    for at, (step, piece_ref) in enumerate(zip(steps, pieces)):
        pool_keys(piece_ref, pk_ref, at, head_size)
        absorb(scale, begins, me, step, piece_ref, q_ref, best_ref, sum_ref, at * blocks)


def late_kernel(scale, gate_scale, direct_steps, late_steps, lengths_ref, q_ref, wk_ref, *refs):
    count = len(late_steps)
    pieces = refs[:count]
    own_best_ref, own_sum_ref, own_pk_ref, pq_ref, proj_ref = refs[count : count + 5]
    best_ref, sum_ref, pk_ref = refs[count + 5 : count + 8]
    targets_ref, sent_ref, pooled_k_ref, key_proj_ref = refs[count + 8 : count + 12]
    late_best_ref, late_sum_ref, late_pk_ref, all_pk_ref, column_ref = refs[count + 12 :]
    heads, rows, head_size = q_ref.shape
    kv = wk_ref.shape[0]
    blocks = rows // BLK
    steps = (0, 1) + tuple(direct_steps) + tuple(late_steps)
    ranks = len(steps)
    block_count = blocks * ranks
    own_rows = heads * blocks
    me = lax.axis_index("ctx")
    begins = doc_begins(lengths_ref)
    for at, (step, piece_ref) in enumerate(zip(late_steps, pieces)):
        absorb(
            scale, begins, me, step, piece_ref, q_ref, late_best_ref, late_sum_ref,
            (at + 1) * blocks,
        )

    for at, piece_ref in enumerate(pieces):
        pool_keys(piece_ref, late_pk_ref, at, head_size)
    for group in range(kv):
        for at, step in enumerate(steps):
            if at < 2:
                value = own_pk_ref[group, at]
            elif at < 2 + len(direct_steps):
                value = pk_ref[group, at - 2]
            else:
                value = late_pk_ref[group, at - 2 - len(direct_steps)]
            all_pk_ref[group, me ^ step] = value
    proj_high, proj_low = halves(proj_ref[...])
    proj = jnp.concatenate([proj_high, proj_high, proj_low], axis=1)
    logits = jnp.zeros((own_rows, block_count), F32)
    row = iota((own_rows, block_count), 0)
    for group in range(kv):
        pooled_k = all_pk_ref[group].reshape(block_count, 3 * head_size).astype(BF16)
        key_proj = dot(pooled_k, wk_ref[group], 1, 0)
        pooled_k_ref[group] = pooled_k
        key_proj_ref[group] = key_proj
        key_high, key_low = halves(key_proj)
        part = dot(proj, jnp.concatenate([key_high, key_low, key_high], axis=1), 1, 1)
        logits = jnp.where(row // (own_rows // kv) == group, part, logits)
    query_block = me * blocks + row % blocks
    key_block = iota((own_rows, block_count), 1)
    allowed = (key_block <= query_block) & (key_block >= start_of(begins, query_block))
    logits = jnp.where(allowed, logits * gate_scale, LOW)
    weights = jnp.exp(logits - jnp.max(logits, axis=1, keepdims=True))
    probs = weights / jnp.sum(weights, axis=1, keepdims=True)

    stat_row = iota((block_count, rows), 0)
    at = stat_row // blocks
    step = jnp.where(at < 2 + len(direct_steps), 2 * (at - 1), 2 * (at - len(direct_steps)) - 1)
    step = jnp.where(at < 2, at, step)
    key_block = (me ^ step) * blocks + stat_row % blocks
    lane_block = me * blocks + iota((block_count, rows), 1) // BLK
    valid = (key_block <= lane_block) & (key_block >= start_of(begins, lane_block))
    lane = iota((block_count, LANES), 1)
    half_lane = lane // BLK
    tile_row = iota((2 * blocks, rows), 0)

    def whole(own, direct, late):
        mixed = jnp.where(tile_row < blocks, direct[-2 * blocks :], late[: 2 * blocks])
        parts = [own, mixed]
        if direct.shape[0] > 2 * blocks:
            parts.insert(1, direct[: -2 * blocks])
        if late.shape[0] > 2 * blocks:
            parts.append(late[2 * blocks :])
        return jnp.concatenate(parts, axis=0)

    columns = jnp.zeros((block_count, LANES), F32)
    for head in range(heads):
        best = whole(own_best_ref[head], best_ref[head], late_best_ref[head])
        total = whole(own_sum_ref[head], sum_ref[head], late_sum_ref[head])
        best = jnp.where(valid, best, LOW)
        shifted = (best - jnp.max(best, axis=0, keepdims=True)) * scale
        total = jnp.sum(jnp.where(valid, total, 0.0) * jnp.exp2(shifted), axis=0, keepdims=True)
        ratio = shifted - jnp.log2(total)
        for block in range(blocks):
            tile = block * BLK // LANES
            inside = half_lane == block % (LANES // BLK)
            part = jnp.where(inside, ratio[:, tile * LANES : (tile + 1) * LANES], LOW)
            high = jnp.max(part, axis=1, keepdims=True)
            columns = jnp.where(lane == head * blocks + block, high, columns)
    raw = jnp.exp2(columns)
    raw = raw * (1.0 / jnp.sum(raw, axis=0, keepdims=True))
    for at, step in enumerate(steps):
        column_ref[me ^ step] = raw[at * blocks : (at + 1) * blocks]
    final = column_ref[...].reshape(block_count, LANES)
    if block_count < LANES:
        final = jnp.concatenate([final, jnp.zeros((LANES - block_count, LANES), F32)], axis=0)
    targets = final.T[0:own_rows, 0:block_count]
    for head in range(heads):
        targets_ref[head] = targets[head * blocks : (head + 1) * blocks]

    delta = jnp.where(allowed, probs - targets, 0.0)
    high, low = halves(delta)
    pieces_of_row = [high.astype(F32), low.astype(F32)]
    width = sent_ref.shape[2]
    if width > 2 * block_count:
        pieces_of_row.append(jnp.zeros((own_rows, width - 2 * block_count), F32))
    pooled_q = pq_ref[...]
    if width > head_size:
        pooled_q = jnp.concatenate(
            [pooled_q, jnp.zeros((own_rows, width - head_size), F32)], axis=1
        )
    packed = jnp.concatenate([pooled_q, jnp.concatenate(pieces_of_row, axis=1)], axis=0)
    packed = packed.astype(BF16)
    for rank in range(ranks):
        sent_ref[rank] = packed


def gate_kernel(
    scale, packed_ref, pooled_k_ref, key_proj_ref, wq_ref, key_grad_ref, wq_grad_ref, wk_grad_ref,
    own_ref,
):
    ranks, packed_rows, _ = packed_ref.shape
    kv, block_count, _ = pooled_k_ref.shape
    heads, head_size, _ = wq_ref.shape
    repeats = heads // kv
    blocks = block_count // ranks
    me = lax.axis_index("ctx")
    packed = packed_ref[...].astype(F32)
    for group in range(kv):
        key_high, key_low = halves(key_proj_ref[group] * scale)
        both_keys = jnp.concatenate([key_high, key_high], axis=0)
        pooled, deltas, projected = [], [], []
        for head in range(group * repeats, (group + 1) * repeats):
            rows = packed[:, head * blocks : (head + 1) * blocks, 0:head_size]
            pooled.append(rows.reshape(block_count, head_size).astype(BF16))
            at = packed_rows // 2 + head * blocks
            rows = packed[:, at : at + blocks, :].reshape(block_count, -1)
            deltas.append(rows[:, 0 : 2 * block_count].astype(BF16))
            projected.append(dot(pooled[-1], wq_ref[head], 1, 0))
        delta = jnp.concatenate(deltas, axis=0)
        delta_high = delta[:, 0:block_count]
        query_grad = dot(delta, both_keys, 1, 0) + dot(delta_high, key_low, 1, 0)
        grad_high, grad_low = halves(query_grad)
        for at in range(repeats):
            rows = slice(at * block_count, (at + 1) * block_count)
            wq_grad_ref[group * repeats + at] = dot(
                jnp.concatenate([pooled[at], pooled[at]], axis=0),
                jnp.concatenate([grad_high[rows], grad_low[rows]], axis=0),
                0,
                0,
            )
        proj_high, proj_low = halves(jnp.concatenate(projected, axis=0) * scale)
        main = dot(delta, proj_high, 0, 0)
        key_grad = main[0:block_count] + main[block_count:] + dot(delta_high, proj_low, 0, 0)
        grad_high, grad_low = halves(key_grad)
        pooled_k = pooled_k_ref[group]
        wk_grad_ref[group] = dot(
            jnp.concatenate([pooled_k, pooled_k], axis=0),
            jnp.concatenate([grad_high, grad_low], axis=0),
            0,
            0,
        )
        own_ref[...] = key_grad.reshape(ranks, blocks, head_size)
        key_grad_ref[:, group, :] = own_ref[me]


def per_device(queries, keys, doc_lengths, gate_query_weight, gate_key_weight):
    rows, heads, head_size = queries.shape
    kv = keys.shape[1]
    ranks = lax.axis_size("ctx")
    blocks = rows // BLK
    block_count = blocks * ranks
    own_rows = heads * blocks
    scale = LOG2E / math.sqrt(head_size)
    gate_scale = 1.0 / math.sqrt(gate_query_weight.shape[2])
    params = pltpu.CompilerParams(vmem_limit_bytes=VMEM_LIMIT)
    smem = pl.BlockSpec(memory_space=pltpu.SMEM)
    vmem = pl.BlockSpec(memory_space=pltpu.VMEM)
    anywhere = pl.BlockSpec(memory_space=pltpu.HBM)

    def near(value):
        return pltpu.with_memory_space_constraint(value, pltpu.VMEM)

    def distant(value):
        return pltpu.with_memory_space_constraint(value, pltpu.HBM)

    def exchange(value, step):
        return lax.ppermute(value, "ctx", [(i, i ^ step) for i in range(ranks)])

    flat_keys = keys.reshape(rows, kv * head_size)
    direct_steps = list(range(2, ranks, 2))
    late_steps = list(range(3, ranks, 2))
    pieces = {0: flat_keys}
    for step in [1] + direct_steps:
        pieces[step] = exchange(flat_keys, step)

    head_queries = queries.transpose(1, 0, 2)
    pool_width = 3 * head_size
    own_stats = pltpu.VMEM((heads, 2 * blocks, rows), F32)
    stats = pltpu.VMEM((heads, ranks // 2 * blocks, rows), F32)
    *near_values, own_best, own_sum, own_pk, pooled_q, proj, ready = pl.pallas_call(
        functools.partial(own_kernel, scale),
        out_shape=(
            pltpu.VMEM(head_queries.shape, BF16),
            pltpu.VMEM(gate_query_weight.shape, BF16),
            own_stats,
            own_stats,
            pltpu.VMEM((kv, 2, blocks, pool_width), F32),
            pltpu.VMEM((own_rows, head_size), F32),
            pltpu.VMEM((own_rows, head_size), F32),
            pltpu.VMEM((8, LANES), F32),
        ),
        in_specs=[smem, anywhere, anywhere, vmem, vmem],
        out_specs=(vmem,) * 8,
        scratch_shapes=[pltpu.SemaphoreType.DMA((2,))],
        compiler_params=params,
        name="own_key_blocks",
    )(doc_lengths, distant(head_queries), distant(gate_query_weight), near(pieces[0]), near(pieces[1]))
    for step in direct_steps[:-1]:
        pieces[step + 1] = exchange(pieces[step], 1)
    far = direct_steps[-1:]
    passed = pl.pallas_call(
        pass_kernel,
        out_shape=tuple(pltpu.VMEM(flat_keys.shape, BF16) for _ in far),
        in_specs=[vmem] * (1 + len(far)),
        out_specs=(vmem,) * len(far),
        input_output_aliases={1 + at: at for at in range(len(far))},
        compiler_params=params,
        name="pass_on",
    )(near(ready), *[near(pieces[s]) for s in far])
    for step, piece in zip(far, passed):
        pieces[step] = piece
        pieces[step + 1] = exchange(piece, 1)
    pieces = {step: near(piece) for step, piece in pieces.items()}
    near_q, near_wq = (near(value) for value in near_values)
    direct = pl.pallas_call(
        functools.partial(direct_kernel, scale, direct_steps),
        out_shape=(
            stats,
            stats,
            pltpu.VMEM((kv, len(direct_steps), blocks, pool_width), F32),
        ),
        in_specs=[smem] + [vmem] * (1 + len(direct_steps)),
        out_specs=(vmem,) * 3,
        compiler_params=params,
        name="direct_key_blocks",
    )(doc_lengths, near_q, *[pieces[s] for s in direct_steps])
    width = -(-2 * block_count // LANES) * LANES
    block_targets, sent, pooled_k, key_proj = pl.pallas_call(
        functools.partial(late_kernel, scale, gate_scale, direct_steps, late_steps),
        out_shape=(
            jax.ShapeDtypeStruct((heads, blocks, block_count), F32),
            pltpu.VMEM((ranks, 2 * own_rows, width), BF16),
            pltpu.VMEM((kv, block_count, pool_width), BF16),
            pltpu.VMEM((kv, block_count, head_size), F32),
        ),
        in_specs=[smem] + [vmem] * (10 + len(late_steps)),
        out_specs=(vmem,) * 4,
        scratch_shapes=[
            stats,
            stats,
            pltpu.VMEM((kv, len(late_steps), blocks, pool_width), F32),
            pltpu.VMEM((kv, ranks, blocks, pool_width), F32),
            pltpu.VMEM((ranks, blocks, LANES), F32),
        ],
        compiler_params=params,
        name="late_key_blocks",
    )(
        doc_lengths,
        near_q,
        near(gate_key_weight),
        *[pieces[s] for s in late_steps],
        *[near(value) for value in (own_best, own_sum, own_pk, pooled_q, proj, *direct)],
    )
    packed = lax.all_to_all(sent, "ctx", 0, 0)
    key_proj_grad, query_weight_grad, key_weight_grad = pl.pallas_call(
        functools.partial(gate_kernel, gate_scale),
        out_shape=(
            jax.ShapeDtypeStruct((blocks, kv, head_size), F32),
            jax.ShapeDtypeStruct(gate_query_weight.shape, F32),
            jax.ShapeDtypeStruct(gate_key_weight.shape, F32),
        ),
        in_specs=[vmem] * 4,
        out_specs=(vmem,) * 3,
        scratch_shapes=[pltpu.VMEM((ranks, blocks, head_size), F32)],
        compiler_params=params,
        name="gate_gradients",
    )(near(packed), near(pooled_k), near(key_proj), near_wq)
    return (block_targets, key_proj_grad, query_weight_grad, key_weight_grad)


def solution(mesh):
    placed = (
        P(("groups", "ctx"), "head", None),
        P(("groups", "ctx"), "head", None),
        P("groups"),
        P("head", None, None),
        P("head", None, None),
    )
    return jax.shard_map(
        per_device,
        mesh=mesh,
        in_specs=placed,
        out_specs=(
            P("head", ("groups", "ctx"), None),
            P(("groups", "ctx"), "head", None),
            P(("groups", "head"), None, None),
            P(("groups", "head"), None, None),
        ),
        check_vma=False,
    )
```

```python
import functools
import math

import jax
import jax.numpy as jnp
from jax import lax
from jax.experimental import pallas as pl
from jax.experimental.pallas import tpu as pltpu
from jax.sharding import PartitionSpec as P

BLK = 64
LANES = 128
LOG2E = 1.4426950408889634
LOW = -1e30
VMEM_LIMIT = 24 * 1024 * 1024
F32 = jnp.float32
BF16 = jnp.bfloat16


def dot(a, b, a_dim, b_dim, precision=None):
    return lax.dot_general(
        a, b, (((a_dim,), (b_dim,)), ((), ())), precision=precision, preferred_element_type=F32
    )


def halves(value):
    high = value.astype(BF16)
    return high, (value - high.astype(F32)).astype(BF16)


def iota(shape, dim):
    return lax.broadcasted_iota(jnp.int32, shape, dim)


def doc_begins(lengths_ref):
    begins, total = [], jnp.int32(0)
    for doc in range(lengths_ref.shape[0]):
        begins.append(total)
        total = total + lengths_ref[doc]
    return begins


def start_of(begins, block):
    start = jnp.zeros_like(block)
    for begin in begins:
        start = jnp.maximum(start, jnp.where(begin <= block, begin, 0))
    return start


def pool_keys(piece_ref, out_ref, at, head_size):
    rows, width = piece_ref.shape
    keys = piece_ref[...].astype(F32).reshape(rows // BLK, BLK, width)
    stats = (jnp.max(keys, 1), jnp.min(keys, 1), jnp.sum(keys, 1) * (1.0 / BLK))
    for group in range(width // head_size):
        for part, value in enumerate(stats):
            out_ref[group, at, :, part * head_size : (part + 1) * head_size] = value[
                :, group * head_size : (group + 1) * head_size
            ]


def absorb(scale, begins, me, step, piece_ref, q_ref, best_ref, sum_ref, at):
    heads, rows, head_size = q_ref.shape
    kv = piece_ref.shape[1] // head_size
    blocks = rows // BLK
    source = me ^ step
    needed = (source <= me) & (source * blocks + blocks > start_of(begins, me * blocks))

    @pl.when(needed)
    def _():
        if step == 0:
            causal = iota((rows, rows), 0) <= iota((rows, rows), 1)
        for head in range(heads):
            group = head // (heads // kv)
            key_rows = piece_ref[:, group * head_size : (group + 1) * head_size]
            scores = dot(key_rows, q_ref[head], 1, 1)
            if step == 0:
                scores = jnp.where(causal, scores, LOW)
            scores = scores.reshape(blocks, BLK, rows)
            best = jnp.max(scores, axis=1)
            best_ref[head, at : at + blocks, :] = best
            sum_ref[head, at : at + blocks, :] = jnp.sum(
                jnp.exp2((scores - best[:, None, :]) * scale), axis=1
            )


def absorb_together(scale, begins, me, steps, pieces, q_ref, best_ref, sum_ref):
    heads, rows, head_size = q_ref.shape
    kv = pieces[0].shape[1] // head_size
    blocks = rows // BLK
    first_needed = start_of(begins, me * blocks)
    needed = False
    for step in steps:
        source = me ^ step
        needed |= (source <= me) & (source * blocks + blocks > first_needed)

    @pl.when(needed)
    def _():
        for group in range(kv):
            lanes = slice(group * head_size, (group + 1) * head_size)
            key_rows = jnp.concatenate([piece_ref[:, lanes] for piece_ref in pieces], axis=0)
            for head in range(group * heads // kv, (group + 1) * heads // kv):
                scores = dot(key_rows, q_ref[head], 1, 1).reshape(-1, BLK, rows)
                best = jnp.max(scores, axis=1)
                best_ref[head] = best
                sum_ref[head] = jnp.sum(
                    jnp.exp2((scores - best[:, None, :]) * scale), axis=1
                )


def own_kernel(
    scale, lengths_ref, far_q_ref, far_wq_ref, own_ref,
    q_ref, wq_ref, best_ref, sum_ref, pk_ref, pq_ref, proj_ref, kept_lengths_ref, copied,
):
    heads, rows, head_size = q_ref.shape
    blocks = rows // BLK
    me = lax.axis_index("ctx")
    begins = doc_begins(lengths_ref)
    q_copy = pltpu.make_async_copy(far_q_ref, q_ref, copied.at[0])
    wq_copy = pltpu.make_async_copy(far_wq_ref, wq_ref, copied.at[1])
    q_copy.start()
    wq_copy.start()
    for doc in range(lengths_ref.shape[0]):
        kept_lengths_ref[doc] = lengths_ref[doc]
    pool_keys(own_ref, pk_ref, 0, head_size)
    q_copy.wait()
    wq_copy.wait()
    for head in range(heads):
        values = q_ref[head].astype(F32).reshape(blocks, BLK, head_size)
        pooled = (jnp.sum(values, axis=1) * (1.0 / BLK)).astype(BF16)
        pq_ref[head * blocks : (head + 1) * blocks, :] = pooled.astype(F32)
        proj_ref[head * blocks : (head + 1) * blocks, :] = dot(pooled, wq_ref[head], 1, 0)
    absorb(scale, begins, me, 0, own_ref, q_ref, best_ref, sum_ref, 0)


def direct_kernel(scale, steps, lengths_ref, q_ref, *refs):
    pieces = refs[: len(steps)]
    best_ref, sum_ref, pk_ref = refs[len(steps) :]
    _, rows, head_size = q_ref.shape
    blocks = rows // BLK
    me = lax.axis_index("ctx")
    begins = doc_begins(lengths_ref)
    for at, (step, piece_ref) in enumerate(zip(steps, pieces)):
        pool_keys(piece_ref, pk_ref, at, head_size)
        absorb(scale, begins, me, step, piece_ref, q_ref, best_ref, sum_ref, at * blocks)


def late_kernel(scale, gate_scale, direct_steps, late_steps, lengths_ref, q_ref, wk_ref, *refs):
    count = len(late_steps)
    pieces = refs[:count]
    own_best_ref, own_sum_ref, own_pk_ref, pq_ref, proj_ref = refs[count : count + 5]
    best_ref, sum_ref, pk_ref = refs[count + 5 : count + 8]
    targets_ref, sent_ref, pooled_k_ref, key_proj_ref = refs[count + 8 : count + 12]
    late_best_ref, late_sum_ref, late_pk_ref, all_pk_ref, column_ref = refs[count + 12 :]
    heads, rows, head_size = q_ref.shape
    kv = wk_ref.shape[0]
    blocks = rows // BLK
    steps = (0,) + tuple(direct_steps) + tuple(late_steps)
    ranks = len(steps)
    block_count = blocks * ranks
    own_rows = heads * blocks
    me = lax.axis_index("ctx")
    begins = doc_begins(lengths_ref)
    absorb_together(
        scale, begins, me, late_steps, pieces, q_ref, late_best_ref, late_sum_ref
    )

    for at, piece_ref in enumerate(pieces):
        pool_keys(piece_ref, late_pk_ref, at, head_size)
    for group in range(kv):
        for at, step in enumerate(steps):
            if at < 1:
                value = own_pk_ref[group, at]
            elif at < 1 + len(direct_steps):
                value = pk_ref[group, at - 1]
            else:
                value = late_pk_ref[group, at - 1 - len(direct_steps)]
            all_pk_ref[group, me ^ step] = value
    proj_high, proj_low = halves(proj_ref[...])
    proj = jnp.concatenate([proj_high, proj_high, proj_low], axis=1)
    logits = jnp.zeros((own_rows, block_count), F32)
    row = iota((own_rows, block_count), 0)
    for group in range(kv):
        pooled_k = all_pk_ref[group].reshape(block_count, 3 * head_size).astype(BF16)
        key_proj = dot(pooled_k, wk_ref[group], 1, 0)
        pooled_k_ref[group] = pooled_k
        key_proj_ref[group] = key_proj
        key_high, key_low = halves(key_proj)
        part = dot(proj, jnp.concatenate([key_high, key_low, key_high], axis=1), 1, 1)
        logits = jnp.where(row // (own_rows // kv) == group, part, logits)
    query_block = me * blocks + row % blocks
    key_block = iota((own_rows, block_count), 1)
    allowed = (key_block <= query_block) & (key_block >= start_of(begins, query_block))
    logits = jnp.where(allowed, logits * gate_scale, LOW)
    weights = jnp.exp(logits - jnp.max(logits, axis=1, keepdims=True))
    probs = weights / jnp.sum(weights, axis=1, keepdims=True)

    stat_row = iota((block_count, rows), 0)
    key_block = (me ^ (stat_row // blocks)) * blocks + stat_row % blocks
    lane_block = me * blocks + iota((block_count, rows), 1) // BLK
    valid = (key_block <= lane_block) & (key_block >= start_of(begins, lane_block))
    lane = iota((block_count, LANES), 1)
    half_lane = lane // BLK
    columns = jnp.zeros((block_count, LANES), F32)
    for head in range(heads):
        best = [own_best_ref[head], best_ref[head], late_best_ref[head]]
        total = [own_sum_ref[head], sum_ref[head], late_sum_ref[head]]
        best, total = jnp.concatenate(best, axis=0), jnp.concatenate(total, axis=0)
        best = jnp.where(valid, best, LOW)
        shifted = (best - jnp.max(best, axis=0, keepdims=True)) * scale
        total = jnp.sum(jnp.where(valid, total, 0.0) * jnp.exp2(shifted), axis=0, keepdims=True)
        ratio = shifted - jnp.log2(total)
        for block in range(blocks):
            tile = block * BLK // LANES
            inside = half_lane == block % (LANES // BLK)
            part = jnp.where(inside, ratio[:, tile * LANES : (tile + 1) * LANES], LOW)
            high = jnp.max(part, axis=1, keepdims=True)
            columns = jnp.where(lane == head * blocks + block, high, columns)
    raw = jnp.exp2(columns)
    raw = raw * (1.0 / jnp.sum(raw, axis=0, keepdims=True))
    for at, step in enumerate(steps):
        column_ref[me ^ step] = raw[at * blocks : (at + 1) * blocks]
    final = column_ref[...].reshape(block_count, LANES)
    if block_count < LANES:
        final = jnp.concatenate([final, jnp.zeros((LANES - block_count, LANES), F32)], axis=0)
    targets = final.T[0:own_rows, 0:block_count]
    for head in range(heads):
        targets_ref[head] = targets[head * blocks : (head + 1) * blocks]

    delta = jnp.where(allowed, probs - targets, 0.0)
    high, low = halves(delta)
    pieces_of_row = [high.astype(F32), low.astype(F32)]
    width = sent_ref.shape[1]
    if width > 2 * block_count:
        pieces_of_row.append(jnp.zeros((own_rows, width - 2 * block_count), F32))
    pooled_q = pq_ref[...]
    if width > head_size:
        pooled_q = jnp.concatenate(
            [pooled_q, jnp.zeros((own_rows, width - head_size), F32)], axis=1
        )
    packed = jnp.concatenate([pooled_q, jnp.concatenate(pieces_of_row, axis=1)], axis=0)
    sent_ref[...] = packed.astype(BF16)


def join_kernel(own_ref, side_ref, joined_ref):
    joined_ref[0] = own_ref[...]
    joined_ref[1] = side_ref[...]


def gate_kernel(scale, count, *refs):
    packed = jnp.concatenate([ref[...].astype(F32) for ref in refs[:count]], axis=0)
    own_targets_ref, pooled_k_ref, key_proj_ref, wq_ref = refs[count : count + 4]
    targets_ref, key_grad_ref, wq_grad_ref, wk_grad_ref, own_ref = refs[count + 4 :]
    targets_ref[...] = own_targets_ref[...]
    ranks, packed_rows, _ = packed.shape
    kv, block_count, _ = pooled_k_ref.shape
    heads, head_size, _ = wq_ref.shape
    repeats = heads // kv
    blocks = block_count // ranks
    me = lax.axis_index("ctx")
    for group in range(kv):
        key_high, key_low = halves(key_proj_ref[group] * scale)
        both_keys = jnp.concatenate([key_high, key_high], axis=0)
        pooled, deltas, projected = [], [], []
        for head in range(group * repeats, (group + 1) * repeats):
            rows = packed[:, head * blocks : (head + 1) * blocks, 0:head_size]
            pooled.append(rows.reshape(block_count, head_size).astype(BF16))
            at = packed_rows // 2 + head * blocks
            rows = packed[:, at : at + blocks, :].reshape(block_count, -1)
            deltas.append(rows[:, 0 : 2 * block_count].astype(BF16))
            projected.append(dot(pooled[-1], wq_ref[head], 1, 0))
        delta = jnp.concatenate(deltas, axis=0)
        delta_high = delta[:, 0:block_count]
        query_grad = dot(delta, both_keys, 1, 0) + dot(delta_high, key_low, 1, 0)
        grad_high, grad_low = halves(query_grad)
        for at in range(repeats):
            rows = slice(at * block_count, (at + 1) * block_count)
            wq_grad_ref[group * repeats + at] = dot(
                jnp.concatenate([pooled[at], pooled[at]], axis=0),
                jnp.concatenate([grad_high[rows], grad_low[rows]], axis=0),
                0,
                0,
            )
        proj_high, proj_low = halves(jnp.concatenate(projected, axis=0) * scale)
        main = dot(delta, proj_high, 0, 0)
        key_grad = main[0:block_count] + main[block_count:] + dot(delta_high, proj_low, 0, 0)
        grad_high, grad_low = halves(key_grad)
        pooled_k = pooled_k_ref[group]
        wk_grad_ref[group] = dot(
            jnp.concatenate([pooled_k, pooled_k], axis=0),
            jnp.concatenate([grad_high, grad_low], axis=0),
            0,
            0,
        )
        own_ref[...] = key_grad.reshape(ranks, blocks, head_size)
        key_grad_ref[:, group, :] = own_ref[me]


def per_device(queries, keys, doc_lengths, gate_query_weight, gate_key_weight):
    rows, heads, head_size = queries.shape
    kv = keys.shape[1]
    ranks = lax.axis_size("ctx")
    blocks = rows // BLK
    block_count = blocks * ranks
    own_rows = heads * blocks
    scale = LOG2E / math.sqrt(head_size)
    gate_scale = 1.0 / math.sqrt(gate_query_weight.shape[2])
    params = pltpu.CompilerParams(vmem_limit_bytes=VMEM_LIMIT)
    smem = pl.BlockSpec(memory_space=pltpu.SMEM)
    vmem = pl.BlockSpec(memory_space=pltpu.VMEM)
    anywhere = pl.BlockSpec(memory_space=pltpu.HBM)

    def near(value):
        return pltpu.with_memory_space_constraint(value, pltpu.VMEM)

    def distant(value):
        return pltpu.with_memory_space_constraint(value, pltpu.HBM)

    def exchange(value, step):
        return lax.ppermute(value, "ctx", [(i, i ^ step) for i in range(ranks)])

    flat_keys = keys.reshape(rows, kv * head_size)
    head_queries = queries.transpose(1, 0, 2)
    pool_width = 3 * head_size
    own_stats = pltpu.VMEM((heads, blocks, rows), F32)
    *near_values, own_best, own_sum, own_pk, pooled_q, proj, lengths = pl.pallas_call(
        functools.partial(own_kernel, scale),
        out_shape=(
            pltpu.VMEM(head_queries.shape, BF16),
            pltpu.VMEM(gate_query_weight.shape, BF16),
            own_stats,
            own_stats,
            pltpu.VMEM((kv, 1, blocks, pool_width), F32),
            pltpu.VMEM((own_rows, head_size), F32),
            pltpu.VMEM((own_rows, head_size), F32),
            pltpu.SMEM(doc_lengths.shape, jnp.int32),
        ),
        in_specs=[smem, anywhere, anywhere, vmem],
        out_specs=(vmem,) * 7 + (smem,),
        scratch_shapes=[pltpu.SemaphoreType.DMA((2,))],
        compiler_params=params,
        name="own_key_blocks",
    )(doc_lengths, distant(head_queries), distant(gate_query_weight), near(flat_keys))
    near_q, near_wq = (near(value) for value in near_values)
    lengths = pltpu.with_memory_space_constraint(lengths, pltpu.SMEM)

    far = ranks // 2
    direct_steps = list(range(1, far + 1))
    late_steps = list(range(far + 1, ranks))
    pieces = {0: flat_keys}
    for step in direct_steps:
        pieces[step] = exchange(flat_keys, step)
    for step in late_steps:
        pieces[step] = exchange(pieces[far], step - far)
    pieces = {step: near(piece) for step, piece in pieces.items()}
    stats = pltpu.VMEM((heads, len(direct_steps) * blocks, rows), F32)
    late_stats = pltpu.VMEM((heads, len(late_steps) * blocks, rows), F32)
    direct = pl.pallas_call(
        functools.partial(direct_kernel, scale, direct_steps),
        out_shape=(
            stats,
            stats,
            pltpu.VMEM((kv, len(direct_steps), blocks, pool_width), F32),
        ),
        in_specs=[smem] + [vmem] * (1 + len(direct_steps)),
        out_specs=(vmem,) * 3,
        compiler_params=params,
        name="direct_key_blocks",
    )(lengths, near_q, *[pieces[s] for s in direct_steps])
    width = -(-2 * block_count // LANES) * LANES
    block_targets, sent, pooled_k, key_proj = pl.pallas_call(
        functools.partial(late_kernel, scale, gate_scale, direct_steps, late_steps),
        out_shape=(
            pltpu.VMEM((heads, blocks, block_count), F32),
            pltpu.VMEM((2 * own_rows, width), BF16),
            pltpu.VMEM((kv, block_count, pool_width), BF16),
            pltpu.VMEM((kv, block_count, head_size), F32),
        ),
        in_specs=[smem] + [vmem] * (10 + len(late_steps)),
        out_specs=(vmem,) * 4,
        scratch_shapes=[
            late_stats,
            late_stats,
            pltpu.VMEM((kv, len(late_steps), blocks, pool_width), F32),
            pltpu.VMEM((kv, ranks, blocks, pool_width), F32),
            pltpu.VMEM((ranks, blocks, LANES), F32),
        ],
        compiler_params=params,
        name="late_key_blocks",
    )(
        lengths,
        near_q,
        near(gate_key_weight),
        *[pieces[s] for s in late_steps],
        *[near(value) for value in (own_best, own_sum, own_pk, pooled_q, proj, *direct)],
    )
    joined = pl.pallas_call(
        join_kernel,
        out_shape=pltpu.VMEM((2, *sent.shape), BF16),
        in_specs=[vmem, vmem],
        out_specs=vmem,
        compiler_params=params,
        name="join_neighbours",
    )(near(sent), near(exchange(sent, 1)))
    packed = [joined] + [exchange(joined, step) for step in range(2, ranks, 2)]
    return pl.pallas_call(
        functools.partial(gate_kernel, gate_scale, len(packed)),
        out_shape=(
            jax.ShapeDtypeStruct((heads, blocks, block_count), F32),
            jax.ShapeDtypeStruct((blocks, kv, head_size), F32),
            jax.ShapeDtypeStruct(gate_query_weight.shape, F32),
            jax.ShapeDtypeStruct(gate_key_weight.shape, F32),
        ),
        in_specs=[vmem] * (4 + len(packed)),
        out_specs=(vmem,) * 4,
        scratch_shapes=[pltpu.VMEM((ranks, blocks, head_size), F32)],
        compiler_params=params,
        name="gate_gradients",
    )(
        *[near(value) for value in packed],
        near(block_targets),
        near(pooled_k),
        near(key_proj),
        near_wq,
    )


def solution(mesh):
    placed = (
        P(("groups", "ctx"), "head", None),
        P(("groups", "ctx"), "head", None),
        P("groups"),
        P("head", None, None),
        P("head", None, None),
    )
    return jax.shard_map(
        per_device,
        mesh=mesh,
        in_specs=placed,
        out_specs=(
            P("head", ("groups", "ctx"), None),
            P(("groups", "ctx"), "head", None),
            P(("groups", "head"), None, None),
            P(("groups", "head"), None, None),
        ),
        check_vma=False,
    )
```

```python
import functools
import math

import jax
import jax.numpy as jnp
from jax import lax
from jax.experimental import pallas as pl
from jax.experimental.pallas import tpu as pltpu
from jax.sharding import PartitionSpec as P

BLK = 64
LANES = 128
LOG2E = 1.4426950408889634
LOW = -1e30
VMEM_LIMIT = 24 * 1024 * 1024
F32 = jnp.float32
BF16 = jnp.bfloat16


def dot(a, b, a_dim, b_dim, precision=None):
    return lax.dot_general(
        a, b, (((a_dim,), (b_dim,)), ((), ())), precision=precision, preferred_element_type=F32
    )


def halves(value):
    high = value.astype(BF16)
    return high, (value - high.astype(F32)).astype(BF16)


def iota(shape, dim):
    return lax.broadcasted_iota(jnp.int32, shape, dim)


def doc_begins(lengths_ref):
    begins, total = [], jnp.int32(0)
    for doc in range(lengths_ref.shape[0]):
        begins.append(total)
        total = total + lengths_ref[doc]
    return begins


def start_of(begins, block):
    start = jnp.zeros_like(block)
    for begin in begins:
        start = jnp.maximum(start, jnp.where(begin <= block, begin, 0))
    return start


def pool_keys(piece_ref, out_ref, at, head_size):
    rows, width = piece_ref.shape
    keys = piece_ref[...].astype(F32).reshape(rows // BLK, BLK, width)
    stats = (jnp.max(keys, 1), jnp.min(keys, 1), jnp.sum(keys, 1) * (1.0 / BLK))
    for group in range(width // head_size):
        for part, value in enumerate(stats):
            out_ref[group, at, :, part * head_size : (part + 1) * head_size] = value[
                :, group * head_size : (group + 1) * head_size
            ]


def absorb(scale, begins, me, step, piece_ref, q_ref, best_ref, sum_ref, at):
    heads, rows, head_size = q_ref.shape
    kv = piece_ref.shape[1] // head_size
    blocks = rows // BLK
    source = me ^ step
    needed = (source <= me) & (source * blocks + blocks > start_of(begins, me * blocks))

    @pl.when(needed)
    def _():
        if step == 0:
            causal = iota((rows, rows), 0) <= iota((rows, rows), 1)
        for head in range(heads):
            group = head // (heads // kv)
            key_rows = piece_ref[:, group * head_size : (group + 1) * head_size]
            scores = dot(key_rows, q_ref[head], 1, 1)
            if step == 0:
                scores = jnp.where(causal, scores, LOW)
            scores = scores.reshape(blocks, BLK, rows)
            best = jnp.max(scores, axis=1)
            best_ref[head, at : at + blocks, :] = best
            sum_ref[head, at : at + blocks, :] = jnp.sum(
                jnp.exp2((scores - best[:, None, :]) * scale), axis=1
            )


def absorb_together(scale, begins, me, steps, pieces, q_ref, best_ref, sum_ref):
    heads, rows, head_size = q_ref.shape
    kv = pieces[0].shape[1] // head_size
    blocks = rows // BLK
    first_needed = start_of(begins, me * blocks)
    needed = False
    for step in steps:
        source = me ^ step
        needed |= (source <= me) & (source * blocks + blocks > first_needed)

    @pl.when(needed)
    def _():
        for group in range(kv):
            lanes = slice(group * head_size, (group + 1) * head_size)
            key_rows = jnp.concatenate([piece_ref[:, lanes] for piece_ref in pieces], axis=0)
            for head in range(group * heads // kv, (group + 1) * heads // kv):
                scores = dot(key_rows, q_ref[head], 1, 1).reshape(-1, BLK, rows)
                best = jnp.max(scores, axis=1)
                best_ref[head] = best
                sum_ref[head] = jnp.sum(
                    jnp.exp2((scores - best[:, None, :]) * scale), axis=1
                )


def own_kernel(
    scale, lengths_ref, far_q_ref, far_wq_ref, own_ref,
    q_ref, wq_ref, best_ref, sum_ref, pk_ref, pq_ref, proj_ref, kept_lengths_ref, copied,
):
    heads, rows, head_size = q_ref.shape
    blocks = rows // BLK
    me = lax.axis_index("ctx")
    begins = doc_begins(lengths_ref)
    q_copy = pltpu.make_async_copy(far_q_ref, q_ref, copied.at[0])
    wq_copy = pltpu.make_async_copy(far_wq_ref, wq_ref, copied.at[1])
    q_copy.start()
    wq_copy.start()
    for doc in range(lengths_ref.shape[0]):
        kept_lengths_ref[doc] = lengths_ref[doc]
    pool_keys(own_ref, pk_ref, 0, head_size)
    q_copy.wait()
    wq_copy.wait()
    for head in range(heads):
        values = q_ref[head].astype(F32).reshape(blocks, BLK, head_size)
        pooled = (jnp.sum(values, axis=1) * (1.0 / BLK)).astype(BF16)
        pq_ref[head * blocks : (head + 1) * blocks, :] = pooled.astype(F32)
        proj_ref[head * blocks : (head + 1) * blocks, :] = dot(pooled, wq_ref[head], 1, 0)
    absorb(scale, begins, me, 0, own_ref, q_ref, best_ref, sum_ref, 0)


def pass_kernel(marker_ref, *refs):
    del marker_ref, refs


def direct_kernel(scale, steps, lengths_ref, q_ref, *refs):
    pieces = refs[: len(steps)]
    best_ref, sum_ref, pk_ref = refs[len(steps) :]
    _, rows, head_size = q_ref.shape
    blocks = rows // BLK
    me = lax.axis_index("ctx")
    begins = doc_begins(lengths_ref)
    for at, (step, piece_ref) in enumerate(zip(steps, pieces)):
        pool_keys(piece_ref, pk_ref, at, head_size)
        absorb(scale, begins, me, step, piece_ref, q_ref, best_ref, sum_ref, at * blocks)


def late_kernel(scale, gate_scale, direct_steps, late_steps, lengths_ref, q_ref, wk_ref, *refs):
    count = len(late_steps)
    pieces = refs[:count]
    own_best_ref, own_sum_ref, own_pk_ref, pq_ref, proj_ref = refs[count : count + 5]
    best_ref, sum_ref, pk_ref = refs[count + 5 : count + 8]
    targets_ref, sent_ref, pooled_k_ref, key_proj_ref = refs[count + 8 : count + 12]
    late_best_ref, late_sum_ref, late_pk_ref, all_pk_ref, column_ref = refs[count + 12 :]
    heads, rows, head_size = q_ref.shape
    kv = wk_ref.shape[0]
    blocks = rows // BLK
    steps = (0,) + tuple(direct_steps) + tuple(late_steps)
    ranks = len(steps)
    block_count = blocks * ranks
    own_rows = heads * blocks
    me = lax.axis_index("ctx")
    begins = doc_begins(lengths_ref)
    absorb_together(
        scale, begins, me, late_steps, pieces, q_ref, late_best_ref, late_sum_ref
    )

    for at, piece_ref in enumerate(pieces):
        pool_keys(piece_ref, late_pk_ref, at, head_size)
    for group in range(kv):
        for at, step in enumerate(steps):
            if at < 1:
                value = own_pk_ref[group, at]
            elif at < 1 + len(direct_steps):
                value = pk_ref[group, at - 1]
            else:
                value = late_pk_ref[group, at - 1 - len(direct_steps)]
            all_pk_ref[group, me ^ step] = value
    proj_high, proj_low = halves(proj_ref[...])
    proj = jnp.concatenate([proj_high, proj_high, proj_low], axis=1)
    logits = jnp.zeros((own_rows, block_count), F32)
    row = iota((own_rows, block_count), 0)
    for group in range(kv):
        pooled_k = all_pk_ref[group].reshape(block_count, 3 * head_size).astype(BF16)
        key_proj = dot(pooled_k, wk_ref[group], 1, 0)
        pooled_k_ref[group] = pooled_k
        key_proj_ref[group] = key_proj
        key_high, key_low = halves(key_proj)
        part = dot(proj, jnp.concatenate([key_high, key_low, key_high], axis=1), 1, 1)
        logits = jnp.where(row // (own_rows // kv) == group, part, logits)
    query_block = me * blocks + row % blocks
    key_block = iota((own_rows, block_count), 1)
    allowed = (key_block <= query_block) & (key_block >= start_of(begins, query_block))
    logits = jnp.where(allowed, logits * gate_scale, LOW)
    weights = jnp.exp(logits - jnp.max(logits, axis=1, keepdims=True))
    probs = weights / jnp.sum(weights, axis=1, keepdims=True)

    stat_row = iota((block_count, rows), 0)
    key_block = (me ^ (stat_row // blocks)) * blocks + stat_row % blocks
    lane_block = me * blocks + iota((block_count, rows), 1) // BLK
    valid = (key_block <= lane_block) & (key_block >= start_of(begins, lane_block))
    lane = iota((block_count, LANES), 1)
    half_lane = lane // BLK
    columns = jnp.zeros((block_count, LANES), F32)
    for head in range(heads):
        best = [own_best_ref[head], best_ref[head], late_best_ref[head]]
        total = [own_sum_ref[head], sum_ref[head], late_sum_ref[head]]
        best, total = jnp.concatenate(best, axis=0), jnp.concatenate(total, axis=0)
        best = jnp.where(valid, best, LOW)
        shifted = (best - jnp.max(best, axis=0, keepdims=True)) * scale
        total = jnp.sum(jnp.where(valid, total, 0.0) * jnp.exp2(shifted), axis=0, keepdims=True)
        ratio = shifted - jnp.log2(total)
        for block in range(blocks):
            tile = block * BLK // LANES
            inside = half_lane == block % (LANES // BLK)
            part = jnp.where(inside, ratio[:, tile * LANES : (tile + 1) * LANES], LOW)
            high = jnp.max(part, axis=1, keepdims=True)
            columns = jnp.where(lane == head * blocks + block, high, columns)
    raw = jnp.exp2(columns)
    raw = raw * (1.0 / jnp.sum(raw, axis=0, keepdims=True))
    for at, step in enumerate(steps):
        column_ref[me ^ step] = raw[at * blocks : (at + 1) * blocks]
    final = column_ref[...].reshape(block_count, LANES)
    if block_count < LANES:
        final = jnp.concatenate([final, jnp.zeros((LANES - block_count, LANES), F32)], axis=0)
    targets = final.T[0:own_rows, 0:block_count]
    for head in range(heads):
        targets_ref[head] = targets[head * blocks : (head + 1) * blocks]

    delta = jnp.where(allowed, probs - targets, 0.0)
    high, low = halves(delta)
    pieces_of_row = [high.astype(F32), low.astype(F32)]
    width = sent_ref.shape[1]
    if width > 2 * block_count:
        pieces_of_row.append(jnp.zeros((own_rows, width - 2 * block_count), F32))
    pooled_q = pq_ref[...]
    if width > head_size:
        pooled_q = jnp.concatenate(
            [pooled_q, jnp.zeros((own_rows, width - head_size), F32)], axis=1
        )
    packed = jnp.concatenate([pooled_q, jnp.concatenate(pieces_of_row, axis=1)], axis=0)
    sent_ref[...] = packed.astype(BF16)


def join_kernel(own_ref, side_ref, joined_ref):
    joined_ref[0] = own_ref[...]
    joined_ref[1] = side_ref[...]


def gate_kernel(scale, count, *refs):
    packed = jnp.concatenate([ref[...].astype(F32) for ref in refs[:count]], axis=0)
    own_targets_ref, pooled_k_ref, key_proj_ref, wq_ref = refs[count : count + 4]
    targets_ref, key_grad_ref, wq_grad_ref, wk_grad_ref, own_ref = refs[count + 4 :]
    targets_ref[...] = own_targets_ref[...]
    ranks, packed_rows, _ = packed.shape
    kv, block_count, _ = pooled_k_ref.shape
    heads, head_size, _ = wq_ref.shape
    repeats = heads // kv
    blocks = block_count // ranks
    me = lax.axis_index("ctx")
    for group in range(kv):
        key_high, key_low = halves(key_proj_ref[group] * scale)
        both_keys = jnp.concatenate([key_high, key_high], axis=0)
        pooled, deltas, projected = [], [], []
        for head in range(group * repeats, (group + 1) * repeats):
            rows = packed[:, head * blocks : (head + 1) * blocks, 0:head_size]
            pooled.append(rows.reshape(block_count, head_size).astype(BF16))
            at = packed_rows // 2 + head * blocks
            rows = packed[:, at : at + blocks, :].reshape(block_count, -1)
            deltas.append(rows[:, 0 : 2 * block_count].astype(BF16))
            projected.append(dot(pooled[-1], wq_ref[head], 1, 0))
        delta = jnp.concatenate(deltas, axis=0)
        delta_high = delta[:, 0:block_count]
        query_grad = dot(delta, both_keys, 1, 0) + dot(delta_high, key_low, 1, 0)
        grad_high, grad_low = halves(query_grad)
        for at in range(repeats):
            rows = slice(at * block_count, (at + 1) * block_count)
            wq_grad_ref[group * repeats + at] = dot(
                jnp.concatenate([pooled[at], pooled[at]], axis=0),
                jnp.concatenate([grad_high[rows], grad_low[rows]], axis=0),
                0,
                0,
            )
        proj_high, proj_low = halves(jnp.concatenate(projected, axis=0) * scale)
        main = dot(delta, proj_high, 0, 0)
        key_grad = main[0:block_count] + main[block_count:] + dot(delta_high, proj_low, 0, 0)
        grad_high, grad_low = halves(key_grad)
        pooled_k = pooled_k_ref[group]
        wk_grad_ref[group] = dot(
            jnp.concatenate([pooled_k, pooled_k], axis=0),
            jnp.concatenate([grad_high, grad_low], axis=0),
            0,
            0,
        )
        own_ref[...] = key_grad.reshape(ranks, blocks, head_size)
        key_grad_ref[:, group, :] = own_ref[me]


def per_device(queries, keys, doc_lengths, gate_query_weight, gate_key_weight):
    rows, heads, head_size = queries.shape
    kv = keys.shape[1]
    ranks = lax.axis_size("ctx")
    blocks = rows // BLK
    block_count = blocks * ranks
    own_rows = heads * blocks
    scale = LOG2E / math.sqrt(head_size)
    gate_scale = 1.0 / math.sqrt(gate_query_weight.shape[2])
    params = pltpu.CompilerParams(vmem_limit_bytes=VMEM_LIMIT)
    smem = pl.BlockSpec(memory_space=pltpu.SMEM)
    vmem = pl.BlockSpec(memory_space=pltpu.VMEM)
    anywhere = pl.BlockSpec(memory_space=pltpu.HBM)

    def near(value):
        return pltpu.with_memory_space_constraint(value, pltpu.VMEM)

    def distant(value):
        return pltpu.with_memory_space_constraint(value, pltpu.HBM)

    def exchange(value, step):
        return lax.ppermute(value, "ctx", [(i, i ^ step) for i in range(ranks)])

    flat_keys = keys.reshape(rows, kv * head_size)
    head_queries = queries.transpose(1, 0, 2)
    pool_width = 3 * head_size
    own_stats = pltpu.VMEM((heads, blocks, rows), F32)
    *near_values, own_best, own_sum, own_pk, pooled_q, proj, lengths = pl.pallas_call(
        functools.partial(own_kernel, scale),
        out_shape=(
            pltpu.VMEM(head_queries.shape, BF16),
            pltpu.VMEM(gate_query_weight.shape, BF16),
            own_stats,
            own_stats,
            pltpu.VMEM((kv, 1, blocks, pool_width), F32),
            pltpu.VMEM((own_rows, head_size), F32),
            pltpu.VMEM((own_rows, head_size), F32),
            pltpu.SMEM(doc_lengths.shape, jnp.int32),
        ),
        in_specs=[smem, anywhere, anywhere, vmem],
        out_specs=(vmem,) * 7 + (smem,),
        scratch_shapes=[pltpu.SemaphoreType.DMA((2,))],
        compiler_params=params,
        name="own_key_blocks",
    )(doc_lengths, distant(head_queries), distant(gate_query_weight), near(flat_keys))
    near_q, near_wq = (near(value) for value in near_values)
    lengths = pltpu.with_memory_space_constraint(lengths, pltpu.SMEM)

    def after(marker, *values):
        return pl.pallas_call(
            pass_kernel,
            out_shape=tuple(pltpu.VMEM(value.shape, BF16) for value in values),
            in_specs=[smem] + [vmem] * len(values),
            out_specs=(vmem,) * len(values),
            input_output_aliases={1 + at: at for at in range(len(values))},
            compiler_params=params,
            name="pass_on",
        )(marker, *[near(value) for value in values])

    far = ranks // 2
    pieces = {0: flat_keys}
    for step in [far, *range(2, far, 2), 1]:
        pieces[step] = exchange(flat_keys, step)
    (pieces[far],) = after(lengths, pieces[far])
    for step in range(3, far, 2):
        pieces[step] = exchange(pieces[step - 1], 1)
    direct_steps = list(range(1, far + 1))
    late_steps = [step for step in range(1, ranks) if step not in direct_steps]
    for step in range(far + 1, ranks):
        pieces[step] = exchange(pieces[far], step - far)
    pieces = {step: near(piece) for step, piece in pieces.items()}
    stats = pltpu.VMEM((heads, len(direct_steps) * blocks, rows), F32)
    late_stats = pltpu.VMEM((heads, len(late_steps) * blocks, rows), F32)
    direct = pl.pallas_call(
        functools.partial(direct_kernel, scale, direct_steps),
        out_shape=(
            stats,
            stats,
            pltpu.VMEM((kv, len(direct_steps), blocks, pool_width), F32),
        ),
        in_specs=[smem] + [vmem] * (1 + len(direct_steps)),
        out_specs=(vmem,) * 3,
        compiler_params=params,
        name="direct_key_blocks",
    )(lengths, near_q, *[pieces[s] for s in direct_steps])
    width = -(-2 * block_count // LANES) * LANES
    block_targets, sent, pooled_k, key_proj = pl.pallas_call(
        functools.partial(late_kernel, scale, gate_scale, direct_steps, late_steps),
        out_shape=(
            pltpu.VMEM((heads, blocks, block_count), F32),
            pltpu.VMEM((2 * own_rows, width), BF16),
            pltpu.VMEM((kv, block_count, pool_width), BF16),
            pltpu.VMEM((kv, block_count, head_size), F32),
        ),
        in_specs=[smem] + [vmem] * (10 + len(late_steps)),
        out_specs=(vmem,) * 4,
        scratch_shapes=[
            late_stats,
            late_stats,
            pltpu.VMEM((kv, len(late_steps), blocks, pool_width), F32),
            pltpu.VMEM((kv, ranks, blocks, pool_width), F32),
            pltpu.VMEM((ranks, blocks, LANES), F32),
        ],
        compiler_params=params,
        name="late_key_blocks",
    )(
        lengths,
        near_q,
        near(gate_key_weight),
        *[pieces[s] for s in late_steps],
        *[near(value) for value in (own_best, own_sum, own_pk, pooled_q, proj, *direct)],
    )
    joined = pl.pallas_call(
        join_kernel,
        out_shape=pltpu.VMEM((2, *sent.shape), BF16),
        in_specs=[vmem, vmem],
        out_specs=vmem,
        compiler_params=params,
        name="join_neighbours",
    )(near(sent), near(exchange(sent, 1)))
    packed = [joined] + [exchange(joined, step) for step in range(2, ranks, 2)]
    return pl.pallas_call(
        functools.partial(gate_kernel, gate_scale, len(packed)),
        out_shape=(
            jax.ShapeDtypeStruct((heads, blocks, block_count), F32),
            jax.ShapeDtypeStruct((blocks, kv, head_size), F32),
            jax.ShapeDtypeStruct(gate_query_weight.shape, F32),
            jax.ShapeDtypeStruct(gate_key_weight.shape, F32),
        ),
        in_specs=[vmem] * (4 + len(packed)),
        out_specs=(vmem,) * 4,
        scratch_shapes=[pltpu.VMEM((ranks, blocks, head_size), F32)],
        compiler_params=params,
        name="gate_gradients",
    )(
        *[near(value) for value in packed],
        near(block_targets),
        near(pooled_k),
        near(key_proj),
        near_wq,
    )


def solution(mesh):
    placed = (
        P(("groups", "ctx"), "head", None),
        P(("groups", "ctx"), "head", None),
        P("groups"),
        P("head", None, None),
        P("head", None, None),
    )
    return jax.shard_map(
        per_device,
        mesh=mesh,
        in_specs=placed,
        out_specs=(
            P("head", ("groups", "ctx"), None),
            P(("groups", "ctx"), "head", None),
            P(("groups", "head"), None, None),
            P(("groups", "head"), None, None),
        ),
        check_vma=False,
    )
```

```python
import functools
import math

import jax
import jax.numpy as jnp
from jax import lax
from jax.experimental import pallas as pl
from jax.experimental.pallas import tpu as pltpu
from jax.sharding import PartitionSpec as P

BLK = 64
LANES = 128
LOG2E = 1.4426950408889634
LOW = -1e30
VMEM_LIMIT = 24 * 1024 * 1024
F32 = jnp.float32
BF16 = jnp.bfloat16


def dot(a, b, a_dim, b_dim, precision=None):
    return lax.dot_general(
        a, b, (((a_dim,), (b_dim,)), ((), ())), precision=precision, preferred_element_type=F32
    )


def halves(value):
    high = value.astype(BF16)
    return high, (value - high.astype(F32)).astype(BF16)


def iota(shape, dim):
    return lax.broadcasted_iota(jnp.int32, shape, dim)


def doc_begins(lengths_ref):
    begins, total = [], jnp.int32(0)
    for doc in range(lengths_ref.shape[0]):
        begins.append(total)
        total = total + lengths_ref[doc]
    return begins


def start_of(begins, block):
    start = jnp.zeros_like(block)
    for begin in begins:
        start = jnp.maximum(start, jnp.where(begin <= block, begin, 0))
    return start


def pool_keys(piece_ref, out_ref, at, head_size):
    rows, width = piece_ref.shape
    keys = piece_ref[...].astype(F32).reshape(rows // BLK, BLK, width)
    stats = (jnp.max(keys, 1), jnp.min(keys, 1), jnp.sum(keys, 1) * (1.0 / BLK))
    for group in range(width // head_size):
        for part, value in enumerate(stats):
            out_ref[group, at, :, part * head_size : (part + 1) * head_size] = value[
                :, group * head_size : (group + 1) * head_size
            ]


def absorb(scale, begins, me, step, piece_ref, q_ref, best_ref, sum_ref, at):
    heads, rows, head_size = q_ref.shape
    kv = piece_ref.shape[1] // head_size
    blocks = rows // BLK
    source = me ^ step
    needed = (source <= me) & (source * blocks + blocks > start_of(begins, me * blocks))

    @pl.when(needed)
    def _():
        if step == 0:
            causal = iota((rows, rows), 0) <= iota((rows, rows), 1)
        for head in range(heads):
            group = head // (heads // kv)
            key_rows = piece_ref[:, group * head_size : (group + 1) * head_size]
            scores = dot(key_rows, q_ref[head], 1, 1)
            if step == 0:
                scores = jnp.where(causal, scores, LOW)
            scores = scores.reshape(blocks, BLK, rows)
            best = jnp.max(scores, axis=1)
            best_ref[head, at : at + blocks, :] = best
            sum_ref[head, at : at + blocks, :] = jnp.sum(
                jnp.exp2((scores - best[:, None, :]) * scale), axis=1
            )


def absorb_together(scale, begins, me, steps, pieces, q_ref, best_ref, sum_ref):
    heads, rows, head_size = q_ref.shape
    kv = pieces[0].shape[1] // head_size
    blocks = rows // BLK
    first_needed = start_of(begins, me * blocks)
    needed = False
    for step in steps:
        source = me ^ step
        needed |= (source <= me) & (source * blocks + blocks > first_needed)

    @pl.when(needed)
    def _():
        for group in range(kv):
            lanes = slice(group * head_size, (group + 1) * head_size)
            key_rows = jnp.concatenate([piece_ref[:, lanes] for piece_ref in pieces], axis=0)
            for head in range(group * heads // kv, (group + 1) * heads // kv):
                scores = dot(key_rows, q_ref[head], 1, 1).reshape(-1, BLK, rows)
                best = jnp.max(scores, axis=1)
                best_ref[head] = best
                sum_ref[head] = jnp.sum(
                    jnp.exp2((scores - best[:, None, :]) * scale), axis=1
                )


def own_kernel(
    scale, lengths_ref, far_q_ref, far_wq_ref, own_ref,
    q_ref, wq_ref, best_ref, sum_ref, pk_ref, pq_ref, proj_ref, kept_lengths_ref, copied,
):
    heads, rows, head_size = q_ref.shape
    blocks = rows // BLK
    me = lax.axis_index("ctx")
    begins = doc_begins(lengths_ref)
    q_copy = pltpu.make_async_copy(far_q_ref, q_ref, copied.at[0])
    wq_copy = pltpu.make_async_copy(far_wq_ref, wq_ref, copied.at[1])
    q_copy.start()
    wq_copy.start()
    for doc in range(lengths_ref.shape[0]):
        kept_lengths_ref[doc] = lengths_ref[doc]
    pool_keys(own_ref, pk_ref, 0, head_size)
    q_copy.wait()
    wq_copy.wait()
    for head in range(heads):
        values = q_ref[head].astype(F32).reshape(blocks, BLK, head_size)
        pooled = (jnp.sum(values, axis=1) * (1.0 / BLK)).astype(BF16)
        pq_ref[head * blocks : (head + 1) * blocks, :] = pooled.astype(F32)
        proj_ref[head * blocks : (head + 1) * blocks, :] = dot(pooled, wq_ref[head], 1, 0)
    absorb(scale, begins, me, 0, own_ref, q_ref, best_ref, sum_ref, 0)


def pass_kernel(marker_ref, *refs):
    del marker_ref, refs


def pieces_kernel(scale, steps, lengths_ref, q_ref, earlier_ref, *refs):
    del earlier_ref
    pieces = refs[: len(steps)]
    best_ref, sum_ref, pk_ref = refs[len(steps) :]
    _, rows, head_size = q_ref.shape
    blocks = rows // BLK
    me = lax.axis_index("ctx")
    begins = doc_begins(lengths_ref)
    for at, piece_ref in enumerate(pieces):
        pool_keys(piece_ref, pk_ref, at, head_size)
    absorb_together(scale, begins, me, steps, pieces, q_ref, best_ref, sum_ref)


def late_kernel(
    scale, gate_scale, first_steps, middle_steps, late_steps, lengths_ref, q_ref, wk_ref, *refs
):
    count = len(late_steps)
    pieces = refs[:count]
    own_best_ref, own_sum_ref, own_pk_ref, pq_ref, proj_ref = refs[count : count + 5]
    first_best_ref, first_sum_ref, first_pk_ref = refs[count + 5 : count + 8]
    middle_best_ref, middle_sum_ref, middle_pk_ref = refs[count + 8 : count + 11]
    targets_ref, sent_ref, pooled_k_ref, key_proj_ref = refs[count + 11 : count + 15]
    late_best_ref, late_sum_ref, late_pk_ref, all_pk_ref, column_ref = refs[count + 15 :]
    heads, rows, head_size = q_ref.shape
    kv = wk_ref.shape[0]
    blocks = rows // BLK
    steps = (0, *middle_steps, *late_steps, *first_steps)
    ranks = len(steps)
    block_count = blocks * ranks
    own_rows = heads * blocks
    me = lax.axis_index("ctx")
    begins = doc_begins(lengths_ref)
    absorb_together(
        scale, begins, me, late_steps, pieces, q_ref, late_best_ref, late_sum_ref
    )

    for at, piece_ref in enumerate(pieces):
        pool_keys(piece_ref, late_pk_ref, at, head_size)
    for group in range(kv):
        pooled = [own_pk_ref[group, 0]]
        for ref in (middle_pk_ref, late_pk_ref, first_pk_ref):
            pooled += [ref[group, at] for at in range(ref.shape[1])]
        for step, value in zip(steps, pooled):
            all_pk_ref[group, me ^ step] = value
    proj_high, proj_low = halves(proj_ref[...])
    proj = jnp.concatenate([proj_high, proj_high, proj_low], axis=1)
    logits = jnp.zeros((own_rows, block_count), F32)
    row = iota((own_rows, block_count), 0)
    for group in range(kv):
        pooled_k = all_pk_ref[group].reshape(block_count, 3 * head_size).astype(BF16)
        key_proj = dot(pooled_k, wk_ref[group], 1, 0)
        pooled_k_ref[group] = pooled_k
        key_proj_ref[group] = key_proj
        key_high, key_low = halves(key_proj)
        part = dot(proj, jnp.concatenate([key_high, key_low, key_high], axis=1), 1, 1)
        logits = jnp.where(row // (own_rows // kv) == group, part, logits)
    query_block = me * blocks + row % blocks
    key_block = iota((own_rows, block_count), 1)
    allowed = (key_block <= query_block) & (key_block >= start_of(begins, query_block))
    logits = jnp.where(allowed, logits * gate_scale, LOW)
    weights = jnp.exp(logits - jnp.max(logits, axis=1, keepdims=True))
    probs = weights / jnp.sum(weights, axis=1, keepdims=True)

    stat_row = iota((block_count, rows), 0)
    step_of_row = jnp.zeros_like(stat_row)
    for at, step in enumerate(steps):
        step_of_row = jnp.where(stat_row // blocks == at, step, step_of_row)
    key_block = (me ^ step_of_row) * blocks + stat_row % blocks
    lane_block = me * blocks + iota((block_count, rows), 1) // BLK
    valid = (key_block <= lane_block) & (key_block >= start_of(begins, lane_block))
    lane = iota((block_count, LANES), 1)
    half_lane = lane // BLK
    columns = jnp.zeros((block_count, LANES), F32)
    for head in range(heads):
        best = (own_best_ref, middle_best_ref, late_best_ref, first_best_ref)
        total = (own_sum_ref, middle_sum_ref, late_sum_ref, first_sum_ref)
        best = jnp.concatenate([ref[head] for ref in best], axis=0)
        total = jnp.concatenate([ref[head] for ref in total], axis=0)
        best = jnp.where(valid, best, LOW)
        shifted = (best - jnp.max(best, axis=0, keepdims=True)) * scale
        total = jnp.sum(jnp.where(valid, total, 0.0) * jnp.exp2(shifted), axis=0, keepdims=True)
        ratio = shifted - jnp.log2(total)
        for block in range(blocks):
            tile = block * BLK // LANES
            inside = half_lane == block % (LANES // BLK)
            part = jnp.where(inside, ratio[:, tile * LANES : (tile + 1) * LANES], LOW)
            high = jnp.max(part, axis=1, keepdims=True)
            columns = jnp.where(lane == head * blocks + block, high, columns)
    raw = jnp.exp2(columns)
    raw = raw * (1.0 / jnp.sum(raw, axis=0, keepdims=True))
    for at, step in enumerate(steps):
        column_ref[me ^ step] = raw[at * blocks : (at + 1) * blocks]
    final = column_ref[...].reshape(block_count, LANES)
    if block_count < LANES:
        final = jnp.concatenate([final, jnp.zeros((LANES - block_count, LANES), F32)], axis=0)
    targets = final.T[0:own_rows, 0:block_count]
    for head in range(heads):
        targets_ref[head] = targets[head * blocks : (head + 1) * blocks]

    delta = jnp.where(allowed, probs - targets, 0.0)
    high, low = halves(delta)
    pieces_of_row = [high.astype(F32), low.astype(F32)]
    width = sent_ref.shape[1]
    if width > 2 * block_count:
        pieces_of_row.append(jnp.zeros((own_rows, width - 2 * block_count), F32))
    pooled_q = pq_ref[...]
    if width > head_size:
        pooled_q = jnp.concatenate(
            [pooled_q, jnp.zeros((own_rows, width - head_size), F32)], axis=1
        )
    packed = jnp.concatenate([pooled_q, jnp.concatenate(pieces_of_row, axis=1)], axis=0)
    sent_ref[...] = packed.astype(BF16)


def join_kernel(own_ref, side_ref, joined_ref):
    joined_ref[0] = own_ref[...]
    joined_ref[1] = side_ref[...]


def gate_kernel(scale, count, *refs):
    packed = jnp.concatenate([ref[...].astype(F32) for ref in refs[:count]], axis=0)
    own_targets_ref, pooled_k_ref, key_proj_ref, wq_ref = refs[count : count + 4]
    targets_ref, key_grad_ref, wq_grad_ref, wk_grad_ref, own_ref = refs[count + 4 :]
    targets_ref[...] = own_targets_ref[...]
    ranks, packed_rows, _ = packed.shape
    kv, block_count, _ = pooled_k_ref.shape
    heads, head_size, _ = wq_ref.shape
    repeats = heads // kv
    blocks = block_count // ranks
    me = lax.axis_index("ctx")
    for group in range(kv):
        key_high, key_low = halves(key_proj_ref[group] * scale)
        both_keys = jnp.concatenate([key_high, key_high], axis=0)
        pooled, deltas, projected = [], [], []
        for head in range(group * repeats, (group + 1) * repeats):
            rows = packed[:, head * blocks : (head + 1) * blocks, 0:head_size]
            pooled.append(rows.reshape(block_count, head_size).astype(BF16))
            at = packed_rows // 2 + head * blocks
            rows = packed[:, at : at + blocks, :].reshape(block_count, -1)
            deltas.append(rows[:, 0 : 2 * block_count].astype(BF16))
            projected.append(dot(pooled[-1], wq_ref[head], 1, 0))
        delta = jnp.concatenate(deltas, axis=0)
        delta_high = delta[:, 0:block_count]
        query_grad = dot(delta, both_keys, 1, 0) + dot(delta_high, key_low, 1, 0)
        grad_high, grad_low = halves(query_grad)
        for at in range(repeats):
            rows = slice(at * block_count, (at + 1) * block_count)
            wq_grad_ref[group * repeats + at] = dot(
                jnp.concatenate([pooled[at], pooled[at]], axis=0),
                jnp.concatenate([grad_high[rows], grad_low[rows]], axis=0),
                0,
                0,
            )
        proj_high, proj_low = halves(jnp.concatenate(projected, axis=0) * scale)
        main = dot(delta, proj_high, 0, 0)
        key_grad = main[0:block_count] + main[block_count:] + dot(delta_high, proj_low, 0, 0)
        grad_high, grad_low = halves(key_grad)
        pooled_k = pooled_k_ref[group]
        wk_grad_ref[group] = dot(
            jnp.concatenate([pooled_k, pooled_k], axis=0),
            jnp.concatenate([grad_high, grad_low], axis=0),
            0,
            0,
        )
        own_ref[...] = key_grad.reshape(ranks, blocks, head_size)
        key_grad_ref[:, group, :] = own_ref[me]


def per_device(queries, keys, doc_lengths, gate_query_weight, gate_key_weight):
    rows, heads, head_size = queries.shape
    kv = keys.shape[1]
    ranks = lax.axis_size("ctx")
    blocks = rows // BLK
    block_count = blocks * ranks
    own_rows = heads * blocks
    scale = LOG2E / math.sqrt(head_size)
    gate_scale = 1.0 / math.sqrt(gate_query_weight.shape[2])
    params = pltpu.CompilerParams(vmem_limit_bytes=VMEM_LIMIT)
    smem = pl.BlockSpec(memory_space=pltpu.SMEM)
    vmem = pl.BlockSpec(memory_space=pltpu.VMEM)
    anywhere = pl.BlockSpec(memory_space=pltpu.HBM)

    def near(value):
        return pltpu.with_memory_space_constraint(value, pltpu.VMEM)

    def distant(value):
        return pltpu.with_memory_space_constraint(value, pltpu.HBM)

    def exchange(value, step):
        return lax.ppermute(value, "ctx", [(i, i ^ step) for i in range(ranks)])

    flat_keys = keys.reshape(rows, kv * head_size)
    head_queries = queries.transpose(1, 0, 2)
    pool_width = 3 * head_size
    own_stats = pltpu.VMEM((heads, blocks, rows), F32)
    *near_values, own_best, own_sum, own_pk, pooled_q, proj, lengths = pl.pallas_call(
        functools.partial(own_kernel, scale),
        out_shape=(
            pltpu.VMEM(head_queries.shape, BF16),
            pltpu.VMEM(gate_query_weight.shape, BF16),
            own_stats,
            own_stats,
            pltpu.VMEM((kv, 1, blocks, pool_width), F32),
            pltpu.VMEM((own_rows, head_size), F32),
            pltpu.VMEM((own_rows, head_size), F32),
            pltpu.SMEM(doc_lengths.shape, jnp.int32),
        ),
        in_specs=[smem, anywhere, anywhere, vmem],
        out_specs=(vmem,) * 7 + (smem,),
        scratch_shapes=[pltpu.SemaphoreType.DMA((2,))],
        compiler_params=params,
        name="own_key_blocks",
    )(doc_lengths, distant(head_queries), distant(gate_query_weight), near(flat_keys))
    near_q, near_wq = (near(value) for value in near_values)
    lengths = pltpu.with_memory_space_constraint(lengths, pltpu.SMEM)

    def after(marker, *values):
        return pl.pallas_call(
            pass_kernel,
            out_shape=tuple(pltpu.VMEM(value.shape, BF16) for value in values),
            in_specs=[smem] + [vmem] * len(values),
            out_specs=(vmem,) * len(values),
            input_output_aliases={1 + at: at for at in range(len(values))},
            compiler_params=params,
            name="pass_on",
        )(marker, *[near(value) for value in values])

    far = ranks // 2
    pieces = {0: flat_keys}
    for step in [far, *range(2, far, 2), 1]:
        pieces[step] = exchange(flat_keys, step)
    (pieces[far],) = after(lengths, pieces[far])
    for step in range(3, far, 2):
        pieces[step] = exchange(pieces[step - 1], 1)
    direct_steps = list(range(1, far + 1))
    middle_steps = [ranks - 1]
    late_steps = list(range(far + 1, ranks - 1))
    for step in range(far + 1, ranks):
        pieces[step] = exchange(pieces[far], step - far)
    pieces = {step: near(piece) for step, piece in pieces.items()}

    def absorb_pieces(steps, earlier, name):
        stats = pltpu.VMEM((heads, len(steps) * blocks, rows), F32)
        values = pl.pallas_call(
            functools.partial(pieces_kernel, scale, steps),
            out_shape=(
                stats,
                stats,
                pltpu.VMEM((kv, len(steps), blocks, pool_width), F32),
            ),
            in_specs=[smem] + [vmem] * (2 + len(steps)),
            out_specs=(vmem,) * 3,
            compiler_params=params,
            name=name,
        )(lengths, near_q, earlier, *[pieces[s] for s in steps])
        return [near(value) for value in values]

    direct = absorb_pieces(direct_steps, near(own_sum), "direct_key_blocks")
    middle = absorb_pieces(middle_steps, direct[0], "middle_key_blocks")
    late_stats = pltpu.VMEM((heads, len(late_steps) * blocks, rows), F32)
    width = -(-2 * block_count // LANES) * LANES
    block_targets, sent, pooled_k, key_proj = pl.pallas_call(
        functools.partial(late_kernel, scale, gate_scale, direct_steps, middle_steps, late_steps),
        out_shape=(
            pltpu.VMEM((heads, blocks, block_count), F32),
            pltpu.VMEM((2 * own_rows, width), BF16),
            pltpu.VMEM((kv, block_count, pool_width), BF16),
            pltpu.VMEM((kv, block_count, head_size), F32),
        ),
        in_specs=[smem] + [vmem] * (13 + len(late_steps)),
        out_specs=(vmem,) * 4,
        scratch_shapes=[
            late_stats,
            late_stats,
            pltpu.VMEM((kv, len(late_steps), blocks, pool_width), F32),
            pltpu.VMEM((kv, ranks, blocks, pool_width), F32),
            pltpu.VMEM((ranks, blocks, LANES), F32),
        ],
        compiler_params=params,
        name="late_key_blocks",
    )(
        lengths,
        near_q,
        near(gate_key_weight),
        *[pieces[s] for s in late_steps],
        *[near(value) for value in (own_best, own_sum, own_pk, pooled_q, proj)],
        *direct,
        *middle,
    )
    joined = pl.pallas_call(
        join_kernel,
        out_shape=pltpu.VMEM((2, *sent.shape), BF16),
        in_specs=[vmem, vmem],
        out_specs=vmem,
        compiler_params=params,
        name="join_neighbours",
    )(near(sent), near(exchange(sent, 1)))
    packed = [joined] + [exchange(joined, step) for step in range(2, ranks, 2)]
    return pl.pallas_call(
        functools.partial(gate_kernel, gate_scale, len(packed)),
        out_shape=(
            jax.ShapeDtypeStruct((heads, blocks, block_count), F32),
            jax.ShapeDtypeStruct((blocks, kv, head_size), F32),
            jax.ShapeDtypeStruct(gate_query_weight.shape, F32),
            jax.ShapeDtypeStruct(gate_key_weight.shape, F32),
        ),
        in_specs=[vmem] * (4 + len(packed)),
        out_specs=(vmem,) * 4,
        scratch_shapes=[pltpu.VMEM((ranks, blocks, head_size), F32)],
        compiler_params=params,
        name="gate_gradients",
    )(
        *[near(value) for value in packed],
        near(block_targets),
        near(pooled_k),
        near(key_proj),
        near_wq,
    )


def solution(mesh):
    placed = (
        P(("groups", "ctx"), "head", None),
        P(("groups", "ctx"), "head", None),
        P("groups"),
        P("head", None, None),
        P("head", None, None),
    )
    return jax.shard_map(
        per_device,
        mesh=mesh,
        in_specs=placed,
        out_specs=(
            P("head", ("groups", "ctx"), None),
            P(("groups", "ctx"), "head", None),
            P(("groups", "head"), None, None),
            P(("groups", "head"), None, None),
        ),
        check_vma=False,
    )
```

```python
import functools
import math

import jax
import jax.numpy as jnp
from jax import lax
from jax.experimental import pallas as pl
from jax.experimental.pallas import tpu as pltpu
from jax.sharding import PartitionSpec as P

BLK = 64
LANES = 128
LOG2E = 1.4426950408889634
LOW = -1e30
VMEM_LIMIT = 24 * 1024 * 1024
F32 = jnp.float32
BF16 = jnp.bfloat16


def dot(a, b, a_dim, b_dim, precision=None):
    return lax.dot_general(
        a, b, (((a_dim,), (b_dim,)), ((), ())), precision=precision, preferred_element_type=F32
    )


def halves(value):
    high = value.astype(BF16)
    return high, (value - high.astype(F32)).astype(BF16)


def iota(shape, dim):
    return lax.broadcasted_iota(jnp.int32, shape, dim)


def doc_begins(lengths_ref):
    begins, total = [], jnp.int32(0)
    for doc in range(lengths_ref.shape[0]):
        begins.append(total)
        total = total + lengths_ref[doc]
    return begins


def start_of(begins, block):
    start = jnp.zeros_like(block)
    for begin in begins:
        start = jnp.maximum(start, jnp.where(begin <= block, begin, 0))
    return start


def pool_keys(piece_ref, out_ref, at, head_size):
    rows, width = piece_ref.shape
    keys = piece_ref[...].astype(F32).reshape(rows // BLK, BLK, width)
    stats = (jnp.max(keys, 1), jnp.min(keys, 1), jnp.sum(keys, 1) * (1.0 / BLK))
    for group in range(width // head_size):
        for part, value in enumerate(stats):
            out_ref[group, at, :, part * head_size : (part + 1) * head_size] = value[
                :, group * head_size : (group + 1) * head_size
            ]


def absorb(scale, begins, me, step, piece_ref, q_ref, best_ref, sum_ref, at):
    heads, rows, head_size = q_ref.shape
    kv = piece_ref.shape[1] // head_size
    blocks = rows // BLK
    source = me ^ step
    needed = (source <= me) & (source * blocks + blocks > start_of(begins, me * blocks))

    @pl.when(needed)
    def _():
        if step == 0:
            causal = iota((rows, rows), 0) <= iota((rows, rows), 1)
        for head in range(heads):
            group = head // (heads // kv)
            key_rows = piece_ref[:, group * head_size : (group + 1) * head_size]
            scores = dot(key_rows, q_ref[head], 1, 1)
            if step == 0:
                scores = jnp.where(causal, scores, LOW)
            scores = scores.reshape(blocks, BLK, rows)
            best = jnp.max(scores, axis=1)
            best_ref[head, at : at + blocks, :] = best
            sum_ref[head, at : at + blocks, :] = jnp.sum(
                jnp.exp2((scores - best[:, None, :]) * scale), axis=1
            )


def absorb_together(scale, begins, me, steps, pieces, q_ref, best_ref, sum_ref):
    heads, rows, head_size = q_ref.shape
    kv = pieces[0].shape[1] // head_size
    blocks = rows // BLK
    first_needed = start_of(begins, me * blocks)
    needed = False
    for step in steps:
        source = me ^ step
        needed |= (source <= me) & (source * blocks + blocks > first_needed)

    @pl.when(needed)
    def _():
        for group in range(kv):
            lanes = slice(group * head_size, (group + 1) * head_size)
            key_rows = jnp.concatenate([piece_ref[:, lanes] for piece_ref in pieces], axis=0)
            for head in range(group * heads // kv, (group + 1) * heads // kv):
                scores = dot(key_rows, q_ref[head], 1, 1).reshape(-1, BLK, rows)
                best = jnp.max(scores, axis=1)
                best_ref[head] = best
                sum_ref[head] = jnp.sum(
                    jnp.exp2((scores - best[:, None, :]) * scale), axis=1
                )


def own_kernel(
    scale, lengths_ref, far_q_ref, far_wq_ref, own_ref,
    q_ref, wq_ref, best_ref, sum_ref, pk_ref, pq_ref, proj_ref, kept_lengths_ref, copied,
):
    heads, rows, head_size = q_ref.shape
    blocks = rows // BLK
    me = lax.axis_index("ctx")
    begins = doc_begins(lengths_ref)
    q_copy = pltpu.make_async_copy(far_q_ref, q_ref, copied.at[0])
    wq_copy = pltpu.make_async_copy(far_wq_ref, wq_ref, copied.at[1])
    q_copy.start()
    wq_copy.start()
    for doc in range(lengths_ref.shape[0]):
        kept_lengths_ref[doc] = lengths_ref[doc]
    pool_keys(own_ref, pk_ref, 0, head_size)
    q_copy.wait()
    wq_copy.wait()
    for head in range(heads):
        values = q_ref[head].astype(F32).reshape(blocks, BLK, head_size)
        pooled = (jnp.sum(values, axis=1) * (1.0 / BLK)).astype(BF16)
        pq_ref[head * blocks : (head + 1) * blocks, :] = pooled.astype(F32)
        proj_ref[head * blocks : (head + 1) * blocks, :] = dot(pooled, wq_ref[head], 1, 0)
    absorb(scale, begins, me, 0, own_ref, q_ref, best_ref, sum_ref, 0)


def pass_kernel(marker_ref, *refs):
    del marker_ref, refs


def pieces_kernel(scale, steps, lengths_ref, q_ref, earlier_ref, *refs):
    del earlier_ref
    pieces = refs[: len(steps)]
    best_ref, sum_ref, pk_ref = refs[len(steps) :]
    _, rows, head_size = q_ref.shape
    blocks = rows // BLK
    me = lax.axis_index("ctx")
    begins = doc_begins(lengths_ref)
    for at, piece_ref in enumerate(pieces):
        pool_keys(piece_ref, pk_ref, at, head_size)
    absorb_together(scale, begins, me, steps, pieces, q_ref, best_ref, sum_ref)


def late_kernel(
    scale, gate_scale, first_steps, middle_steps, late_steps, lengths_ref, q_ref, wk_ref, *refs
):
    count = len(late_steps)
    pieces = refs[:count]
    own_best_ref, own_sum_ref, own_pk_ref, pq_ref, proj_ref = refs[count : count + 5]
    first_best_ref, first_sum_ref, first_pk_ref = refs[count + 5 : count + 8]
    middle_best_ref, middle_sum_ref, middle_pk_ref = refs[count + 8 : count + 11]
    targets_ref, sent_ref, pooled_k_ref, key_proj_ref = refs[count + 11 : count + 15]
    late_best_ref, late_sum_ref, late_pk_ref, all_pk_ref, column_ref = refs[count + 15 :]
    heads, rows, head_size = q_ref.shape
    kv = wk_ref.shape[0]
    blocks = rows // BLK
    steps = (0, *middle_steps, *late_steps, *first_steps)
    ranks = len(steps)
    block_count = blocks * ranks
    own_rows = heads * blocks
    me = lax.axis_index("ctx")
    begins = doc_begins(lengths_ref)
    absorb_together(
        scale, begins, me, late_steps, pieces, q_ref, late_best_ref, late_sum_ref
    )

    for at, piece_ref in enumerate(pieces):
        pool_keys(piece_ref, late_pk_ref, at, head_size)
    for group in range(kv):
        pooled = [own_pk_ref[group, 0]]
        for ref in (middle_pk_ref, late_pk_ref, first_pk_ref):
            pooled += [ref[group, at] for at in range(ref.shape[1])]
        for step, value in zip(steps, pooled):
            all_pk_ref[group, me ^ step] = value
    proj_high, proj_low = halves(proj_ref[...])
    proj = jnp.concatenate([proj_high, proj_high, proj_low], axis=1)
    logits = jnp.zeros((own_rows, block_count), F32)
    row = iota((own_rows, block_count), 0)
    for group in range(kv):
        pooled_k = all_pk_ref[group].reshape(block_count, 3 * head_size).astype(BF16)
        key_proj = dot(pooled_k, wk_ref[group], 1, 0)
        pooled_k_ref[group] = pooled_k
        key_proj_ref[group] = key_proj
        key_high, key_low = halves(key_proj)
        part = dot(proj, jnp.concatenate([key_high, key_low, key_high], axis=1), 1, 1)
        logits = jnp.where(row // (own_rows // kv) == group, part, logits)
    query_block = me * blocks + row % blocks
    key_block = iota((own_rows, block_count), 1)
    allowed = (key_block <= query_block) & (key_block >= start_of(begins, query_block))
    logits = jnp.where(allowed, logits * gate_scale, LOW)
    weights = jnp.exp(logits - jnp.max(logits, axis=1, keepdims=True))
    probs = weights / jnp.sum(weights, axis=1, keepdims=True)

    stat_row = iota((block_count, rows), 0)
    step_of_row = jnp.zeros_like(stat_row)
    for at, step in enumerate(steps):
        step_of_row = jnp.where(stat_row // blocks == at, step, step_of_row)
    key_block = (me ^ step_of_row) * blocks + stat_row % blocks
    lane_block = me * blocks + iota((block_count, rows), 1) // BLK
    valid = (key_block <= lane_block) & (key_block >= start_of(begins, lane_block))
    lane = iota((block_count, LANES), 1)
    half_lane = lane // BLK
    columns = jnp.zeros((block_count, LANES), F32)
    for head in range(heads):
        best = (own_best_ref, middle_best_ref, late_best_ref, first_best_ref)
        total = (own_sum_ref, middle_sum_ref, late_sum_ref, first_sum_ref)
        best = jnp.concatenate([ref[head] for ref in best], axis=0)
        total = jnp.concatenate([ref[head] for ref in total], axis=0)
        best = jnp.where(valid, best, LOW)
        shifted = (best - jnp.max(best, axis=0, keepdims=True)) * scale
        total = jnp.sum(jnp.where(valid, total, 0.0) * jnp.exp2(shifted), axis=0, keepdims=True)
        ratio = shifted - jnp.log2(total)
        for block in range(blocks):
            tile = block * BLK // LANES
            inside = half_lane == block % (LANES // BLK)
            part = jnp.where(inside, ratio[:, tile * LANES : (tile + 1) * LANES], LOW)
            high = jnp.max(part, axis=1, keepdims=True)
            columns = jnp.where(lane == head * blocks + block, high, columns)
    raw = jnp.exp2(columns)
    raw = raw * (1.0 / jnp.sum(raw, axis=0, keepdims=True))
    for at, step in enumerate(steps):
        column_ref[me ^ step] = raw[at * blocks : (at + 1) * blocks]
    final = column_ref[...].reshape(block_count, LANES)
    if block_count < LANES:
        final = jnp.concatenate([final, jnp.zeros((LANES - block_count, LANES), F32)], axis=0)
    targets = final.T[0:own_rows, 0:block_count]
    for head in range(heads):
        targets_ref[head] = targets[head * blocks : (head + 1) * blocks]

    delta = jnp.where(allowed, probs - targets, 0.0)
    high, low = halves(delta)
    pieces_of_row = [high.astype(F32), low.astype(F32)]
    width = sent_ref.shape[1]
    if width > 2 * block_count:
        pieces_of_row.append(jnp.zeros((own_rows, width - 2 * block_count), F32))
    pooled_q = pq_ref[...]
    if width > head_size:
        pooled_q = jnp.concatenate(
            [pooled_q, jnp.zeros((own_rows, width - head_size), F32)], axis=1
        )
    packed = jnp.concatenate([pooled_q, jnp.concatenate(pieces_of_row, axis=1)], axis=0)
    sent_ref[...] = packed.astype(BF16)


def join_kernel(own_ref, side_ref, joined_ref):
    joined_ref[0] = own_ref[...]
    joined_ref[1] = side_ref[...]


def gate_kernel(scale, count, *refs):
    packed = jnp.concatenate([ref[...].astype(F32) for ref in refs[:count]], axis=0)
    own_targets_ref, pooled_k_ref, key_proj_ref, wq_ref = refs[count : count + 4]
    targets_out, key_grad_out, wq_grad_out, wk_grad_out = refs[count + 4 : count + 8]
    own_ref, key_grad_ref, wq_grad_ref, wk_grad_ref, sent = refs[count + 8 :]
    copies = [pltpu.make_async_copy(own_targets_ref, targets_out, sent.at[0])]
    copies[0].start()
    ranks, packed_rows, _ = packed.shape
    kv, block_count, _ = pooled_k_ref.shape
    heads, head_size, _ = wq_ref.shape
    repeats = heads // kv
    blocks = block_count // ranks
    me = lax.axis_index("ctx")
    for group in range(kv):
        key_high, key_low = halves(key_proj_ref[group] * scale)
        both_keys = jnp.concatenate([key_high, key_high], axis=0)
        pooled, deltas, projected = [], [], []
        for head in range(group * repeats, (group + 1) * repeats):
            rows = packed[:, head * blocks : (head + 1) * blocks, 0:head_size]
            pooled.append(rows.reshape(block_count, head_size).astype(BF16))
            at = packed_rows // 2 + head * blocks
            rows = packed[:, at : at + blocks, :].reshape(block_count, -1)
            deltas.append(rows[:, 0 : 2 * block_count].astype(BF16))
            projected.append(dot(pooled[-1], wq_ref[head], 1, 0))
        delta = jnp.concatenate(deltas, axis=0)
        delta_high = delta[:, 0:block_count]
        query_grad = dot(delta, both_keys, 1, 0) + dot(delta_high, key_low, 1, 0)
        grad_high, grad_low = halves(query_grad)
        for at in range(repeats):
            rows = slice(at * block_count, (at + 1) * block_count)
            wq_grad_ref[group * repeats + at] = dot(
                jnp.concatenate([pooled[at], pooled[at]], axis=0),
                jnp.concatenate([grad_high[rows], grad_low[rows]], axis=0),
                0,
                0,
            )
        proj_high, proj_low = halves(jnp.concatenate(projected, axis=0) * scale)
        main = dot(delta, proj_high, 0, 0)
        key_grad = main[0:block_count] + main[block_count:] + dot(delta_high, proj_low, 0, 0)
        grad_high, grad_low = halves(key_grad)
        pooled_k = pooled_k_ref[group]
        wk_grad_ref[group] = dot(
            jnp.concatenate([pooled_k, pooled_k], axis=0),
            jnp.concatenate([grad_high, grad_low], axis=0),
            0,
            0,
        )
        own_ref[...] = key_grad.reshape(ranks, blocks, head_size)
        key_grad_ref[:, group, :] = own_ref[me]
        heads_here = pl.ds(group * repeats, repeats)
        copies += [
            pltpu.make_async_copy(
                wq_grad_ref.at[heads_here], wq_grad_out.at[heads_here], sent.at[2 + 2 * group]
            ),
            pltpu.make_async_copy(
                wk_grad_ref.at[group], wk_grad_out.at[group], sent.at[3 + 2 * group]
            ),
        ]
        copies[-2].start()
        copies[-1].start()
    copies.append(pltpu.make_async_copy(key_grad_ref, key_grad_out, sent.at[1]))
    copies[-1].start()
    for copy in copies:
        copy.wait()


def per_device(queries, keys, doc_lengths, gate_query_weight, gate_key_weight):
    rows, heads, head_size = queries.shape
    kv = keys.shape[1]
    ranks = lax.axis_size("ctx")
    blocks = rows // BLK
    block_count = blocks * ranks
    own_rows = heads * blocks
    scale = LOG2E / math.sqrt(head_size)
    gate_scale = 1.0 / math.sqrt(gate_query_weight.shape[2])
    params = pltpu.CompilerParams(vmem_limit_bytes=VMEM_LIMIT)
    smem = pl.BlockSpec(memory_space=pltpu.SMEM)
    vmem = pl.BlockSpec(memory_space=pltpu.VMEM)
    anywhere = pl.BlockSpec(memory_space=pltpu.HBM)

    def near(value):
        return pltpu.with_memory_space_constraint(value, pltpu.VMEM)

    def distant(value):
        return pltpu.with_memory_space_constraint(value, pltpu.HBM)

    def exchange(value, step):
        return lax.ppermute(value, "ctx", [(i, i ^ step) for i in range(ranks)])

    flat_keys = keys.reshape(rows, kv * head_size)
    head_queries = queries.transpose(1, 0, 2)
    pool_width = 3 * head_size
    own_stats = pltpu.VMEM((heads, blocks, rows), F32)
    *near_values, own_best, own_sum, own_pk, pooled_q, proj, lengths = pl.pallas_call(
        functools.partial(own_kernel, scale),
        out_shape=(
            pltpu.VMEM(head_queries.shape, BF16),
            pltpu.VMEM(gate_query_weight.shape, BF16),
            own_stats,
            own_stats,
            pltpu.VMEM((kv, 1, blocks, pool_width), F32),
            pltpu.VMEM((own_rows, head_size), F32),
            pltpu.VMEM((own_rows, head_size), F32),
            pltpu.SMEM(doc_lengths.shape, jnp.int32),
        ),
        in_specs=[smem, anywhere, anywhere, vmem],
        out_specs=(vmem,) * 7 + (smem,),
        scratch_shapes=[pltpu.SemaphoreType.DMA((2,))],
        compiler_params=params,
        name="own_key_blocks",
    )(doc_lengths, distant(head_queries), distant(gate_query_weight), near(flat_keys))
    near_q, near_wq = (near(value) for value in near_values)
    lengths = pltpu.with_memory_space_constraint(lengths, pltpu.SMEM)

    def after(marker, *values):
        return pl.pallas_call(
            pass_kernel,
            out_shape=tuple(pltpu.VMEM(value.shape, BF16) for value in values),
            in_specs=[smem] + [vmem] * len(values),
            out_specs=(vmem,) * len(values),
            input_output_aliases={1 + at: at for at in range(len(values))},
            compiler_params=params,
            name="pass_on",
        )(marker, *[near(value) for value in values])

    far = ranks // 2
    pieces = {0: flat_keys}
    for step in [far, *range(2, far, 2), 1]:
        pieces[step] = exchange(flat_keys, step)
    (pieces[far],) = after(lengths, pieces[far])
    for step in range(3, far, 2):
        pieces[step] = exchange(pieces[step - 1], 1)
    direct_steps = list(range(1, far + 1))
    middle_steps = [ranks - 1]
    late_steps = list(range(far + 1, ranks - 1))
    for step in range(far + 1, ranks):
        pieces[step] = exchange(pieces[far], step - far)
    pieces = {step: near(piece) for step, piece in pieces.items()}

    def absorb_pieces(steps, earlier, name):
        stats = pltpu.VMEM((heads, len(steps) * blocks, rows), F32)
        values = pl.pallas_call(
            functools.partial(pieces_kernel, scale, steps),
            out_shape=(
                stats,
                stats,
                pltpu.VMEM((kv, len(steps), blocks, pool_width), F32),
            ),
            in_specs=[smem] + [vmem] * (2 + len(steps)),
            out_specs=(vmem,) * 3,
            compiler_params=params,
            name=name,
        )(lengths, near_q, earlier, *[pieces[s] for s in steps])
        return [near(value) for value in values]

    direct = absorb_pieces(direct_steps, near(own_sum), "direct_key_blocks")
    middle = absorb_pieces(middle_steps, direct[0], "middle_key_blocks")
    late_stats = pltpu.VMEM((heads, len(late_steps) * blocks, rows), F32)
    width = -(-2 * block_count // LANES) * LANES
    block_targets, sent, pooled_k, key_proj = pl.pallas_call(
        functools.partial(late_kernel, scale, gate_scale, direct_steps, middle_steps, late_steps),
        out_shape=(
            pltpu.VMEM((heads, blocks, block_count), F32),
            pltpu.VMEM((2 * own_rows, width), BF16),
            pltpu.VMEM((kv, block_count, pool_width), BF16),
            pltpu.VMEM((kv, block_count, head_size), F32),
        ),
        in_specs=[smem] + [vmem] * (13 + len(late_steps)),
        out_specs=(vmem,) * 4,
        scratch_shapes=[
            late_stats,
            late_stats,
            pltpu.VMEM((kv, len(late_steps), blocks, pool_width), F32),
            pltpu.VMEM((kv, ranks, blocks, pool_width), F32),
            pltpu.VMEM((ranks, blocks, LANES), F32),
        ],
        compiler_params=params,
        name="late_key_blocks",
    )(
        lengths,
        near_q,
        near(gate_key_weight),
        *[pieces[s] for s in late_steps],
        *[near(value) for value in (own_best, own_sum, own_pk, pooled_q, proj)],
        *direct,
        *middle,
    )
    joined = pl.pallas_call(
        join_kernel,
        out_shape=pltpu.VMEM((2, *sent.shape), BF16),
        in_specs=[vmem, vmem],
        out_specs=vmem,
        compiler_params=params,
        name="join_neighbours",
    )(near(sent), near(exchange(sent, 1)))
    packed = [joined] + [exchange(joined, step) for step in range(2, ranks, 2)]
    return pl.pallas_call(
        functools.partial(gate_kernel, gate_scale, len(packed)),
        out_shape=(
            jax.ShapeDtypeStruct((heads, blocks, block_count), F32),
            jax.ShapeDtypeStruct((blocks, kv, head_size), F32),
            jax.ShapeDtypeStruct(gate_query_weight.shape, F32),
            jax.ShapeDtypeStruct(gate_key_weight.shape, F32),
        ),
        in_specs=[vmem] * (4 + len(packed)),
        out_specs=(anywhere,) * 4,
        scratch_shapes=[
            pltpu.VMEM((ranks, blocks, head_size), F32),
            pltpu.VMEM((blocks, kv, head_size), F32),
            pltpu.VMEM(gate_query_weight.shape, F32),
            pltpu.VMEM(gate_key_weight.shape, F32),
            pltpu.SemaphoreType.DMA((2 + 2 * kv,)),
        ],
        compiler_params=params,
        name="gate_gradients",
    )(
        *[near(value) for value in packed],
        near(block_targets),
        near(pooled_k),
        near(key_proj),
        near_wq,
    )


def solution(mesh):
    placed = (
        P(("groups", "ctx"), "head", None),
        P(("groups", "ctx"), "head", None),
        P("groups"),
        P("head", None, None),
        P("head", None, None),
    )
    return jax.shard_map(
        per_device,
        mesh=mesh,
        in_specs=placed,
        out_specs=(
            P("head", ("groups", "ctx"), None),
            P(("groups", "ctx"), "head", None),
            P(("groups", "head"), None, None),
            P(("groups", "head"), None, None),
        ),
        check_vma=False,
    )
```
